256 devices in a mesh: seq: 16 (over z, y_lo), chan: 16 (over x, y_hi, core).
Axes of the slice: x: 4, y: 4 (y_hi: 2, y_lo: 2; y = y_hi * 2 + y_lo), z: 8, core: 2. Of those that a mesh axis runs over, the one named last changes fastest.
Arguments:
- hidden_in: bfloat16 [8192, 4096], P('seq', 'chan'), may hold values from -6 to 6
- in_weight: bfloat16 [3, 4096, 2048], P(None, None, 'chan'), may hold values from -0.09375 to 0.09375
- conv_taps: float32 [3, 3, 2048], P(None, None, 'chan'), may hold values from -3 to 3
- decay_rate: float32 [16, 2048], P(None, 'chan'), may hold values from 0.0002 to 0.05
- mode_angle: float32 [16, 2048], P(None, 'chan'), may hold values from -3.140625 to 3.140625
- residue: float32 [2, 16, 2048], P(None, None, 'chan'), may hold values from -0.2 to 0.2
- skip_gain: float32 [2048], P('chan'), may hold values from -5 to 5
- out_grad: float32 [2048, 8192], P('chan', 'seq'), may hold values from -6 to 6
Outputs:
- mixed_out: float32 [2048, 8192], P('chan', 'seq')
- input_grad: float32 [8192, 4096], P('seq', 'chan')
- weight_grad: float32 [3, 4096, 2048], P(None, 'seq', 'chan')
- taps_grad: float32 [3, 3, 2048], P(None, None, 'chan')
- residue_grad: float32 [2, 16, 2048], P(None, None, 'chan')
- skip_grad: float32 [2048], P('chan')
The draws below stay inside these ranges and needn't reach their ends.
All inputs are finite; a program needn't handle non-finite values.
Results may differ from the reference program's by a relative error of at most 0.0029.
Values may be sent and summed in bfloat16 or wider, within the bound.
No kernel may reach another device: no remote copies, remote signals or barrier semaphores. Data moves between devices by JAX's collectives and lax.ppermute only.
A program may use at most 128 MiB of HBM per device.

```python
import math
import jax
import jax.numpy as jnp
from jax import lax

D = 4096
C = 2048
MODES = 16
TOKENS = 8192


def block_scale(key, extent, shards, least, high):
    gain, own = 1.0, jax.random.fold_in(key, 6)
    for dim, parts in shards:
        draws = jnp.exp(jax.random.uniform(jax.random.fold_in(own, dim), (parts,), jnp.float32, least / len(shards), high / len(shards)))
        gain = gain * jnp.repeat(draws, extent[dim] // parts).reshape([-1 if axis == dim else 1 for axis in range(len(extent))])
    return gain


def centred(own_key, dims, deviation, bound, pieces=(), held_as=jnp.bfloat16):
    array = jax.random.normal(own_key, dims, jnp.float32) * deviation
    if len(pieces) > 0:
        array = block_scale(own_key, dims, pieces, -0.22, 0.18) * array
    return jnp.clip(array, min=-bound, max=bound).astype(held_as)


def setup_inputs(seed: int = 0) -> dict:
    seeds = jax.random.split(jax.random.key(seed), 9)
    return {
        "hidden_in": centred(seeds[0], (TOKENS, D), 1.0, 6.0, ((0, 16), (1, 16))),
        "in_weight": centred(seeds[1], (3, D, C), D ** -0.5, 0.09375, ((2, 16),)),
        "conv_taps": centred(seeds[2], (3, 3, C), 0.6, 3.0, ((2, 16),), jnp.float32),
        "decay_rate": jnp.clip(jnp.exp(math.log(0.05) - 5.521461 * jax.random.uniform(seeds[3], (MODES, C), jnp.float32) ** block_scale(seeds[3], (MODES, C), ((1, 16),), -0.2, 0.2)), 0.0002, 0.05),
        "mode_angle": jnp.clip(jax.random.uniform(seeds[4], (MODES, C), jnp.float32, -3.140625, 3.140625), -3.140625, 3.140625),
        "residue": centred(seeds[5], (2, MODES, C), 0.03, 0.2, ((2, 16),), jnp.float32),
        "skip_gain": centred(seeds[6], (C,), 1.0, 5.0, ((0, 16),), jnp.float32),
        "out_grad": centred(seeds[7], (C, TOKENS), 1.0, 6.0, ((0, 16), (1, 16)), jnp.float32),
    }


def shift_taps(padded, taps, count):
    return sum(taps[:, offset, :, None] * padded[:, :, 2 - offset:2 - offset + count] for offset in range(3))


def reference(hidden_in, in_weight, conv_taps, decay_rate, mode_angle, residue, skip_gain, out_grad):
    length = hidden_in.shape[0]
    inputs = hidden_in.astype(jnp.float32)
    weights = in_weight.astype(jnp.float32)
    proj = jnp.einsum('td,kdc->kct', inputs, weights)
    padded = jnp.pad(proj, ((0, 0), (0, 0), (2, 0)))
    branches = shift_taps(padded, conv_taps, length)
    query_branch = branches[0]
    key_branch = branches[1]
    value_branch = branches[2]
    product = key_branch * value_branch
    positions = jnp.arange(length, dtype=jnp.float32)

    def add_mode(total, params):
        rate_row, angle_row, real_row, imag_row = params
        fading = jnp.exp(-rate_row[:, None] * positions)
        decay_cos = fading * jnp.cos(angle_row[:, None] * positions)
        decay_sin = fading * jnp.sin(angle_row[:, None] * positions)
        return total + (real_row[:, None] * decay_cos - imag_row[:, None] * decay_sin), None

    response, _ = lax.scan(add_mode, jnp.zeros_like(product), (decay_rate, mode_angle, residue[0], residue[1]))
    padlen = 2 * length
    prod_spec = jnp.fft.rfft(product, n=padlen, axis=1)
    filt_spec = jnp.fft.rfft(response, n=padlen, axis=1)
    long_conv = jnp.fft.irfft(prod_spec * filt_spec, n=padlen, axis=1)[:, :length]
    long_out = long_conv + skip_gain[:, None] * product
    mixed_out = query_branch * long_out
    grad_long = out_grad * query_branch
    grad_query = out_grad * long_out
    grad_spec = jnp.fft.rfft(grad_long, n=padlen, axis=1)
    grad_prod = jnp.fft.irfft(jnp.conj(filt_spec) * grad_spec, n=padlen, axis=1)[:, :length]
    grad_prod = grad_prod + skip_gain[:, None] * grad_long
    grad_resp = jnp.fft.irfft(grad_spec * jnp.conj(prod_spec), n=padlen, axis=1)[:, :length]
    skip_grad = jnp.sum(grad_long * product, axis=1)

    def mode_grads(params):
        rate_row, angle_row = params
        fading = jnp.exp(-rate_row[:, None] * positions)
        decay_cos = fading * jnp.cos(angle_row[:, None] * positions)
        decay_sin = fading * jnp.sin(angle_row[:, None] * positions)
        return jnp.sum(grad_resp * decay_cos, axis=1), -jnp.sum(grad_resp * decay_sin, axis=1)

    real_grad, imag_grad = lax.map(mode_grads, (decay_rate, mode_angle))
    residue_grad = jnp.stack([real_grad, imag_grad])
    grad_branches = jnp.stack([grad_query, grad_prod * value_branch, grad_prod * key_branch])
    padded_back = jnp.pad(grad_branches, ((0, 0), (0, 0), (0, 2)))
    grad_proj = sum(conv_taps[:, offset, :, None] * padded_back[:, :, offset:offset + length] for offset in range(3))
    taps_grad = jnp.stack([jnp.sum(grad_branches * padded[:, :, 2 - offset:2 - offset + length], axis=2) for offset in range(3)], axis=1)
    grad_low = lax.optimization_barrier(grad_proj.astype(jnp.bfloat16)).astype(jnp.float32)
    input_grad = jnp.einsum('kct,kdc->td', grad_low, weights)
    weight_grad = jnp.einsum('td,kct->kdc', inputs, grad_low)
    return mixed_out, input_grad, weight_grad, taps_grad, residue_grad, skip_grad
```

```python
import jax
import jax.numpy as jnp
from jax import lax
from jax.experimental import pallas as pl
from jax.experimental.pallas import tpu as pltpu
from jax.sharding import PartitionSpec as P

F32 = jnp.float32
BF16 = jnp.bfloat16
MODES = 16
SUB = 64
ROWS = 8 * SUB
EXT = ROWS + 8


def chan_pairs(dx, dy, dc):
    pairs = []
    for c in range(16):
        x, y, core = c // 4, c // 2 % 2, c % 2
        pairs.append((c, (x + dx) % 4 * 4 + (y + dy) % 2 * 2 + (core + dc) % 2))
    return pairs


def seq_pairs(dz, dy):
    return [(s, (s // 2 + dz) % 8 * 2 + (s % 2 + dy) % 2) for s in range(16)]


def to_chan(x, dx, dy, dc=0):
    return lax.ppermute(x, "chan", chan_pairs(dx, dy, dc))


def to_seq(x, dz, dy=0):
    return lax.ppermute(x, "seq", seq_pairs(dz, dy))


def pole_power(rate, angle, count):
    high = jnp.round(angle * 1024.0) * (1.0 / 1024.0)
    low = angle - high
    one, two = high * count, low * count
    mag = jnp.exp(-rate * count)
    cos1, sin1, cos2, sin2 = jnp.cos(one), jnp.sin(one), jnp.cos(two), jnp.sin(two)
    return mag * (cos1 * cos2 - sin1 * sin2), mag * (sin1 * cos2 + cos1 * sin2)


def spread(pair):
    both = jnp.concatenate(pair, axis=0)
    return jnp.broadcast_to(both[:, None, :], (2 * MODES, 8, both.shape[1]))


def times(a, b):
    return a[0] * b[0] - a[1] * b[1], a[0] * b[1] + a[1] * b[0]


def copy_all(pairs, sems):
    copies = [pltpu.make_async_copy(a, b, sems.at[i]) for i, (a, b) in enumerate(pairs)]
    for c in copies:
        c.start()
    return copies


def wait_all(copies, start=False):
    for c in copies:
        if start:
            c.start()
        c.wait()


def stream(sources, weight_far, par, held, weight, sems):
    copies = []
    for b in range(8):
        pairs = [(weight_far.at[:, b, par], weight.at[:, b])]
        pairs += [(src.at[b], dst.at[b]) for src, dst in zip(sources, held)]
        group = [pltpu.make_async_copy(f, t, sems.at[6 * b + i]) for i, (f, t) in enumerate(pairs)]
        for c in group:
            c.start()
        copies.append(group)
    return copies


def columns(weight, b):
    return jnp.concatenate([weight[k, b] for k in range(3)], axis=1)


def convolve(taps, ext, k):
    lanes = slice(128 * k, 128 * k + 128)
    total = taps[3 * k : 3 * k + 1, :] * ext[8 : 8 + ROWS, lanes]
    total = total + taps[3 * k + 1 : 3 * k + 2, :] * ext[7 : 7 + ROWS, lanes]
    return total + taps[3 * k + 2 : 3 * k + 3, :] * ext[6 : 6 + ROWS, lanes]


def half_kernel(at, mine_far, weight_far, out, mine, weight, made, sems):
    copies = stream([mine_far], weight_far, at[0], [mine], weight, sems)
    for b in range(0, 8, 4):
        for i in range(b, b + 4):
            wait_all(copies[i])
        left = jnp.concatenate([mine[i] for i in range(b, b + 4)], axis=1)
        right = jnp.concatenate([columns(weight, i) for i in range(b, b + 4)], axis=0)
        total = jnp.dot(left, right, preferred_element_type=F32)
        made[...] = total if b == 0 else made[...] + total
    wait_all([pltpu.make_async_copy(made, out, sems.at[0])], start=True)


def states_kernel(
    at, other_far, weight_far, half, taps, og, lam, pwf, pwb,
    ext, prod, gl, st, send, other, weight, ends, sems, io,
):
    seq = at[2]
    copies = stream([other_far], weight_far, 1 - at[0], [other], weight, sems)
    for b in range(0, 8, 4):
        for i in range(b, b + 4):
            wait_all(copies[i])
        left = jnp.concatenate([other[i] for i in range(b, b + 4)], axis=1)
        right = jnp.concatenate([columns(weight, i) for i in range(b, b + 4)], axis=0)
        total = jnp.dot(left, right, preferred_element_type=F32)
        if b == 0:
            io.need(0)
        ext[8:520, :] = (half[...] if b == 0 else ext[8:520, :]) + total
    ext[0:8, :] = jnp.zeros((8, 384), F32)
    ext[520:528, :] = jnp.zeros((8, 384), F32)
    io.done(0)
    io.need(1, 2)
    q, k, v = (convolve(taps, ext, i) for i in range(3))
    fresh = lax.broadcasted_iota(jnp.int32, (ROWS, 128), 0) >= 2
    prod[...] = jnp.where(fresh, k * v, 0.0)
    gl[...] = jnp.where(fresh, og[0:ROWS, :] * q, 0.0)
    io.done(1, 2)
    edge = [k[0:2], v[0:2], q[0:2], og[0:2, :]]
    edge += [ext[518:520, 128 * i : 128 * i + 128] for i in range(3)]
    edge = jnp.concatenate(edge + [jnp.zeros((2, 128), F32)], axis=0)
    io.need(3, 4, 5)
    half = MODES // 2
    for src, powers, back, base in ((prod, pwf, False, 0), (gl, pwb, True, 32)):
        for n0 in range(0, MODES, half):

            def body(step, carry, n0=n0, back=back, src=src):
                i = SUB - 1 - step if back else step
                v = src[pl.ds(i, 8, stride=SUB), :]
                out = []
                for k in range(half):
                    re, im = carry[2 * k], carry[2 * k + 1]
                    lr, li = lam[n0 + k], lam[MODES + n0 + k]
                    out += [re * lr - im * li + v, re * li + im * lr]
                return tuple(out)

            zero = tuple(jnp.zeros((8, 128), F32) for _ in range(2 * half))
            carry = lax.fori_loop(0, SUB, body, zero, unroll=4)
            for k in range(half):
                n = n0 + k
                re, im = carry[2 * k], carry[2 * k + 1]
                st[base + n] = re
                st[base + MODES + n] = im
                er, ei = times((re, im), (powers[n], powers[MODES + n]))
                ends[base + n : base + n + 1, :] = jnp.sum(er, axis=0, keepdims=True)
                ends[base + MODES + n : base + MODES + n + 1, :] = jnp.sum(ei, axis=0, keepdims=True)
    io.done(3)
    for j in range(16):
        send[j, 0:32, :] = jnp.where(j >= seq, ends[0:32, :], ends[32:64, :])
        send[j, 32:48, :] = edge


def scan_kernel(prod, gl, st, lam, rho, lam64, y, gp, sums):
    half = MODES // 2
    place = lax.broadcasted_iota(jnp.int32, (8, 128), 0)
    for base, back in ((0, False), (32, True)):
        for n in range(MODES):

            def shift(v, by, back=back):
                moved = pltpu.roll(v, 8 - by if back else by, 0)
                return jnp.where(place < 8 - by if back else place >= by, moved, 0.0)

            re, im = shift(st[base + n], 1), shift(st[base + MODES + n], 1)
            for level, by in enumerate((1, 2, 4)):
                ar, ai = times(
                    (shift(re, by), shift(im, by)), (lam64[32 * level + n], lam64[32 * level + MODES + n])
                )
                re, im = re + ar, im + ai
            sums[32 + base + n] = re
            sums[32 + base + MODES + n] = im
    for n0 in range(0, MODES, half):

        def forward(step, carry, n0=n0):
            p = prod[pl.ds(step, 8, stride=SUB), :]
            g = gl[pl.ds(step, 8, stride=SUB), :]
            out = []
            total = None
            for k in range(half):
                re, im, sr, si = carry[4 * k : 4 * k + 4]
                lr, li = lam[n0 + k], lam[MODES + n0 + k]
                re, im = re * lr - im * li + p, re * li + im * lr
                term = re * rho[n0 + k] - im * rho[MODES + n0 + k]
                total = term if total is None else total + term
                out += [re, im, sr + g * re, si + g * im]
            y[step] = total if n0 == 0 else y[step] + total
            return tuple(out)

        zero = tuple(jnp.zeros((8, 128), F32) for _ in range(4 * half))
        carry = lax.fori_loop(0, SUB, forward, zero, unroll=4)
        for k in range(half):
            sums[n0 + k] = carry[4 * k + 2]
            sums[MODES + n0 + k] = carry[4 * k + 3]

        def backward(step, carry, n0=n0):
            i = SUB - 1 - step
            g = gl[pl.ds(i, 8, stride=SUB), :]
            out = []
            total = None
            for k in range(half):
                re, im = carry[2 * k : 2 * k + 2]
                lr, li = lam[n0 + k], lam[MODES + n0 + k]
                re, im = re * lr - im * li + g, re * li + im * lr
                term = re * rho[n0 + k] - im * rho[MODES + n0 + k]
                total = term if total is None else total + term
                out += [re, im]
            gp[i] = total if n0 == 0 else gp[i] + total
            return tuple(out)

        zero = tuple(jnp.zeros((8, 128), F32) for _ in range(2 * half))
        lax.fori_loop(0, SUB, backward, zero, unroll=4)


def grads_kernel(
    at, arrived, wt, consts, lam, rho, pwf, pwb, y, gp, sums, st, ext, taps, og,
    mixed, low, yt, gt, gb, br, prod, gl, small, io,
):
    seq = at[2]

    def pair(ref, start):
        return ref[start : start + MODES, :], ref[start + MODES : start + 2 * MODES, :]

    io.need(0, 1, 2, 12)
    lam16, inv16, rho16, lam512 = pair(consts, 0), pair(consts, 32), pair(consts, 64), pair(consts, 96)
    lam511, lam510 = pair(consts, 128), pair(consts, 160)
    zero16 = jnp.zeros((MODES, 128), F32)
    s_in, u_in = (zero16, zero16), (zero16, zero16)
    zero2 = jnp.zeros((2, 128), F32)
    own = nxt = [zero2] * 6
    rim = [zero2] * 3
    first = lax.broadcasted_iota(jnp.int32, (2, 128), 0) == 0

    def choose(flag, new, old):
        return [jnp.where(flag, a, b) for a, b in zip(new, old)]

    before = [zero2] * 3
    for j in range(16):
        tilde = arrived[j, 32:40, :]
        kvq = []
        for k, rows in ((1, tilde[0:2]), (2, tilde[2:4]), (0, tilde[4:6])):
            t1, t2 = taps[3 * k + 1 : 3 * k + 2, :], taps[3 * k + 2 : 3 * k + 3, :]
            p2, p1 = before[k][0:1], before[k][1:2]
            kvq.append(rows + jnp.where(first, t1 * p1 + t2 * p2, t2 * p1))
        out_grad = tilde[6:8]
        product = kvq[0] * kvq[1]
        cotangent = out_grad * kvq[2]
        mine = kvq + [out_grad, product, cotangent]
        tail = arrived[j, 40:48, :]
        before = [tail[0:2], tail[2:4], tail[4:6]]
        own = choose(j == seq, mine, own)
        nxt = choose(j == seq + 1, mine, nxt)
        rim = choose(j == seq - 1, before, rim)
        got = pair(arrived.at[j], 0)
        p0, p1 = product[0:1], product[1:2]
        g0, g1 = cotangent[0:1], cotangent[1:2]
        ahead = j < seq
        fixed = [
            got[i] + jnp.where(ahead, lam511[i] * p0 + lam510[i] * p1, lam16[i] * g1 + (g0 if i == 0 else 0.0))
            for i in range(2)
        ]
        re, im = times(fixed, (wt[j, 0:MODES, :], wt[j, MODES : 2 * MODES, :]))
        behind = j > seq
        s_in = (s_in[0] + jnp.where(ahead, re, 0.0), s_in[1] + jnp.where(ahead, im, 0.0))
        u_in = (u_in[0] + jnp.where(behind, re, 0.0), u_in[1] + jnp.where(behind, im, 0.0))

    def read_out(state):
        return jnp.sum(rho16[0] * state[0] - rho16[1] * state[1], axis=0, keepdims=True)

    p0, p1, g0, g1 = own[4][0:1], own[4][1:2], own[5][0:1], own[5][1:2]
    x0 = times(lam16, s_in)
    x0 = (x0[0] + p0, x0[1])
    x1 = times(lam16, x0)
    x1 = (x1[0] + p1, x1[1])
    small[0:16, :] = g0 * x0[0] + g1 * x1[0]
    small[16:32, :] = -(g0 * x0[1] + g1 * x1[1])
    inv2 = times(inv16, inv16)
    s_in = tuple(s_in[i] + inv16[i] * p0 + inv2[i] * p1 for i in range(2))
    carried = times(lam512, s_in)
    last = pair(arrived.at[seq], 0)
    last = (last[0] + carried[0], last[1] + carried[1])
    for extra in range(2):
        moved = times(lam16, last)
        last = (moved[0] + nxt[4][extra : extra + 1], moved[1])
        yt[ROWS + extra : ROWS + extra + 1, :] = read_out(last)
    gt[ROWS : ROWS + 1, :] = read_out(u_in)
    later = times(inv16, (u_in[0] - nxt[5][0:1], u_in[1]))
    gt[ROWS + 1 : ROWS + 2, :] = read_out(later)
    yt[ROWS + 2 : EXT, :] = jnp.zeros((EXT - ROWS - 2, 128), F32)
    gt[ROWS + 2 : EXT, :] = jnp.zeros((EXT - ROWS - 2, 128), F32)
    io.need(3, 4, 5, 6, 7, 8, 9, 10)

    half = MODES // 2
    for n0 in range(0, MODES, half):
        start_f, start_b = [], []
        for k in range(half):
            n = n0 + k
            l8 = (lam[n], lam[MODES + n])
            r8 = (rho[n], rho[MODES + n])

            def full(state, powers, base, n=n):
                wide = tuple(jnp.broadcast_to(s[n : n + 1, :], (8, 128)) for s in state)
                add = times(wide, (powers[n], powers[MODES + n]))
                return times((sums[base + n] + add[0], sums[base + MODES + n] + add[1]), l8)

            q = full(s_in, pwb, 32)
            rr, ri = times(q, (st[32 + n], st[48 + n]))
            small[n : n + 1, :] += jnp.sum(sums[n] + rr, axis=0, keepdims=True)
            small[MODES + n : MODES + n + 1, :] -= jnp.sum(sums[MODES + n] + ri, axis=0, keepdims=True)
            start_f += list(times(q, r8))
            start_b += list(times(full(u_in, pwf, 64), r8))

        def follow(src, dst, back, start, n0=n0):
            def body(step, carry):
                i = SUB - 1 - step if back else step
                at = pl.ds(i, 8, stride=SUB)
                total = src[i] if n0 == 0 else dst[at, :]
                out = []
                for k in range(half):
                    re, im = carry[2 * k], carry[2 * k + 1]
                    total = total + re
                    lr, li = lam[n0 + k], lam[MODES + n0 + k]
                    out += [re * lr - im * li, re * li + im * lr]
                dst[at, :] = total
                return tuple(out)

            lax.fori_loop(0, SUB, body, tuple(start), unroll=4)

        follow(y, yt, False, start_f)
        follow(gp, gt, True, start_b)

    none, one = (jnp.ones_like(zero16), zero16), lam16
    yt[0:1, :] -= read_out(inv16) * p1
    gt[0:1, :] += read_out(none) * g0 + read_out(one) * g1
    gt[1:2, :] += read_out(none) * g1

    io.need(11, 13)
    for k in range(3):
        ext[6:8, 128 * k : 128 * k + 128] = rim[k]
    og[ROWS : ROWS + 2, :] = nxt[3]
    for k, at_k in ((0, 2), (1, 0), (2, 1)):
        lanes = slice(128 * k, 128 * k + 128)
        br[0:ROWS, lanes] = convolve(taps, ext, k)
        br[ROWS : ROWS + 2, lanes] = nxt[at_k]
    br[ROWS + 2 : EXT, :] = jnp.zeros((EXT - ROWS - 2, 384), F32)
    prod[...] = br[:, 128:256] * br[:, 256:384]
    gl[...] = og[...] * br[:, 0:128]
    gain = consts[192:193, :]
    long_out = yt[...] + gain * prod[...]
    gb[:, 0:128] = og[...] * long_out
    grad_prod = gt[...] + gain * gl[...]
    gb[:, 128:256] = grad_prod * br[:, 256:384]
    gb[:, 256:384] = grad_prod * br[:, 128:256]
    for k in range(3):
        lanes = slice(128 * k, 128 * k + 128)
        total = None
        for j in range(3):
            term = taps[3 * k + j : 3 * k + j + 1, :] * gb[j : j + ROWS, lanes]
            total = term if total is None else total + term
            row = 32 + 3 * k + j
            small[row : row + 1, :] = jnp.sum(
                gb[0:ROWS, lanes] * ext[8 - j : 8 - j + ROWS, lanes], axis=0, keepdims=True
            )
        low[0:ROWS, lanes] = total.astype(BF16)
    small[41:42, :] = jnp.sum(gl[0:ROWS, :] * prod[0:ROWS, :], axis=0, keepdims=True)
    small[42:48, :] = jnp.zeros((6, 128), F32)
    wide = jnp.concatenate([small[16 * i : 16 * i + 16, :] for i in range(3)], axis=1)
    high = wide.astype(BF16)
    low[ROWS : ROWS + 16, :] = high
    low[ROWS + 16 :, :] = (wide - high.astype(F32)).astype(BF16)
    io.done(1)
    mixed[...] = (br[0:ROWS, 0:128] * long_out[0:ROWS, :]).T


def turn_kernel(at, a, b, *rest):
    out, held, turned, sems = rest[-4:]

    def run(src):
        copies = copy_all([(src.at[i], held.at[i]) for i in range(8)], sems)
        sent = []
        for i in range(8):
            copies[i].wait()
            turned[i] = held[i].T
            sent += [pltpu.make_async_copy(turned.at[i], out.at[i], sems.at[8 + i])]
            sent[i].start()
        wait_all(sent)

    @pl.when(at[3] == 1)
    def _():
        run(a)

    @pl.when(at[3] == 0)
    def _():
        run(b)


def input_kernel(at, low, low_core, weight, partner, *rest):
    outs, (left, lturn, right, parts, sems) = rest[:8], rest[8:]
    core, x, y = at[0], at[4], at[5]
    copies = copy_all([(low.at[0:ROWS], left.at[0]), (low_core.at[0:ROWS], left.at[1])], sems)
    places = []
    for r in range(8):
        dx, dy = r // 2, r % 2
        places.append((x + dx) % 4 * 2 + (y + dy) % 2)
    order = [1, 2, 3, 4, 5, 6, 7, 0]
    far = []
    for n, r in enumerate(order):
        for s, src in enumerate((weight, partner)):
            c = pltpu.make_async_copy(
                src.at[:, places[r], core], right.at[r, s], sems.at[2 + 2 * n + s]
            )
            c.start()
            far.append(c)
    wait_all(copies)
    lturn[...] = jnp.concatenate([left[0].T, left[1].T], axis=0)
    sent = []
    for n, r in enumerate(order):
        wait_all(far[2 * n : 2 * n + 2])
        cols = jnp.concatenate([right[r, s, k] for s in range(2) for k in range(3)], axis=1)
        parts[r] = jnp.dot(cols, lturn[...], preferred_element_type=F32).astype(BF16)
        c = pltpu.make_async_copy(parts.at[r], outs[r], sems.at[18 + r])
        c.start()
        sent.append(c)
    wait_all(sent)


def weight_kernel(at, kept, given, passed, low, low_y, *rest):
    out, kv, pv, cols, parts, sems = rest[-6:]
    copies = copy_all([(low, cols.at[0]), (low_y, cols.at[1])], sems)
    far = []
    for i in range(8):
        c = pltpu.make_async_copy(kept.at[i], kv.at[i], sems.at[2 + 2 * i])
        c.start()
        far.append(c)
        for flag, src in ((1, given), (0, passed)):
            c = pltpu.make_async_copy(src.at[i], pv.at[i], sems.at[3 + 2 * i])

            @pl.when(at[3] == flag)
            def _(c=c):
                c.start()

        far.append(c)
    wait_all(copies)
    total = jnp.zeros((16, 384), F32)
    for i in range(2):
        for r in (ROWS, ROWS + 16):
            total = total + cols[i, r : r + 16, :].astype(F32)
    high = total.astype(BF16)
    rest_low = (total - high.astype(F32)).astype(BF16)
    sent = []
    for i in range(8):
        wait_all(far[2 * i : 2 * i + 2])
        total = jnp.dot(kv[i], cols[0, 0:ROWS, :], preferred_element_type=F32)
        total = total + lax.dot_general(
            pv[i], cols[1, 0:ROWS, :], (((0,), (0,)), ((), ())), preferred_element_type=F32
        )
        parts[i, 0:256, :] = total.astype(BF16)
        parts[i, 256:272, :] = high
        parts[i, 272:288, :] = rest_low
        c = pltpu.make_async_copy(parts.at[i], out.at[i], sems.at[18 + i])
        c.start()
        sent.append(c)
    wait_all(sent)


def fold_input_kernel(own, *rest):
    parts, out = rest[:-1], rest[-1]
    total = own[...].astype(F32)
    for p in parts:
        total = total + p[...].astype(F32)
    out[...] = total.T


def fold_kernel(parts, out, small):
    for k in range(3):
        lanes = slice(128 * k, 128 * k + 128)
        total = parts[0, :, lanes].astype(F32)
        for j in range(1, 8):
            total = total + parts[j, :, lanes].astype(F32)
        out[k] = total[0:256]
        small[16 * k : 16 * k + 16, :] = total[256:272] + total[272:288]


FAR = pl.BlockSpec(memory_space=pltpu.HBM)
SCALARS = pl.BlockSpec(memory_space=pltpu.SMEM)


def raw_call(kernel, us, outs, scratch, sems, args, in_specs, out_specs):
    return pl.pallas_call(
        kernel,
        in_specs=in_specs,
        out_specs=out_specs,
        out_shape=[jax.ShapeDtypeStruct(s, t) for s, t in outs],
        scratch_shapes=[pltpu.VMEM(s, t) for s, t in scratch] + [pltpu.SemaphoreType.DMA((sems,))],
        compiler_params=pltpu.CompilerParams(vmem_limit_bytes=62 * 1024 * 1024),
        cost_estimate=pl.CostEstimate(flops=int(us * 1.1e9), bytes_accessed=0, transcendentals=0),
    )(*args)


def far_call(kernel, us, at, outs, scratch, sems, *args):
    scalars = () if at is None else (at,)
    specs = [SCALARS] * len(scalars) + [FAR] * len(args)
    return raw_call(kernel, us, outs, scratch, sems, scalars + args, specs, [FAR] * len(outs))


class Staged:
    def __init__(self, ins, outs):
        self.ins, self.outs, self.here, self.gone = ins, outs, set(), set()

    def need(self, *which):
        for i in which:
            if i not in self.here:
                self.here.add(i)
                self.ins[i].wait()

    def done(self, *which):
        for i in which:
            if i not in self.gone:
                self.gone.add(i)
                self.outs[i].start()


def call(kernel, us, at, outs, scratch, *args, far=(), sems=0, late=(), staged=False):
    scalars = () if at is None else (at,)
    n_s, n_f, n_i, n_l, n_o = len(scalars), len(far), len(args), len(late), len(outs)

    def body(*refs):
        refs = list(refs)

        def take(count):
            head = refs[:count]
            del refs[:count]
            return head

        top, far_refs, ins, _, results = take(n_s), take(n_f), take(n_i), take(n_l), take(n_o)
        held, made, own, sem = take(n_i), take(n_o), refs[:-1], refs[-1]

        def copies(pairs, base):
            return [pltpu.make_async_copy(a, b, sem.at[base + i]) for i, (a, b) in enumerate(pairs)]

        coming = copies(zip(ins, held), sems)
        for c in coming:
            c.start()
        io = Staged(coming, copies(zip(made, results), sems + n_i))
        if not staged:
            io.need(*range(n_i))
        extra = ((sem,) if far else ()) + ((io,) if staged else ())
        kernel(*top, *far_refs, *held, *made, *own, *extra)
        io.need(*range(n_i))
        io.done(*range(n_o))
        wait_all(io.outs)

    buffers = [(a.shape, a.dtype) for a in args] + list(outs) + list(scratch)
    specs = [SCALARS] * n_s + [FAR] * (n_f + n_i + n_l)
    total = sems + n_i + n_o
    return raw_call(
        body, us, outs, buffers, total, scalars + tuple(far) + args + tuple(late), specs, [FAR] * n_o
    )


def after(x, *deps):
    return pl.pallas_call(
        lambda *_: None,
        in_specs=[FAR] * (1 + len(deps)),
        out_specs=FAR,
        out_shape=jax.ShapeDtypeStruct(x.shape, x.dtype),
        input_output_aliases={0: 0},
    )(x, *deps)


CHIPS = [[x * 4 + y * 2 + c for x in range(4) for y in range(2)] for c in range(2)]
COLUMNS = [[z * 2 + y for z in range(8)] for y in range(2)]


def exchange(x, axis, groups=None):
    return lax.all_to_all(
        x, axis, split_axis=0, concat_axis=0, tiled=True, axis_index_groups=groups
    )


def joint_pairs(kind):
    pairs = []
    for s in range(16):
        for c in range(16):
            wanted = s % 2 == c % 2
            if kind == "give" and not wanted:
                pairs.append((s * 16 + c, (s ^ 1) * 16 + c))
            if kind == "pass" and wanted:
                pairs.append((s * 16 + c, s * 16 + (c ^ 1)))
    return pairs


def on_device(
    hidden_in, in_weight, conv_taps, decay_rate, mode_angle, residue, skip_gain, out_grad
):
    chan, seq = lax.axis_index("chan"), lax.axis_index("seq")
    core, yl = chan % 2, seq % 2
    same = (yl == core).astype(jnp.int32)
    at = jnp.stack([core, chan, seq, same, chan // 4, chan // 2 % 2]).astype(jnp.int32)

    mine = exchange(jnp.broadcast_to(hidden_in[None], (8, ROWS, 256)), "chan", CHIPS)
    partner = to_chan(in_weight, 0, 0, 1)

    def power(count):
        return pole_power(decay_rate, mode_angle, count)

    lam = power(1.0)
    lam8 = spread(lam)
    rho8 = spread((residue[0], residue[1]))
    eighth = jnp.arange(8, dtype=F32)[None, :, None] * float(SUB)
    sub_rate, sub_angle = decay_rate[:, None, :], mode_angle[:, None, :]
    pwb = jnp.concatenate(pole_power(sub_rate, sub_angle, eighth), axis=0)
    pwf = jnp.concatenate(pole_power(sub_rate, sub_angle, float(7 * SUB) - eighth), axis=0)
    lam64 = jnp.concatenate([spread(power(float(SUB * d))) for d in (1, 2, 4)], axis=0)
    source = jnp.arange(16, dtype=jnp.int32)
    away = jnp.abs(source - seq).astype(F32)[:, None, None] - 1.0
    away = jnp.maximum(away, 0.0) * float(ROWS)
    wt = jnp.concatenate(pole_power(decay_rate[None], mode_angle[None], away), axis=1)
    consts = jnp.concatenate(
        lam + power(-1.0) + (residue[0], residue[1]) + power(float(ROWS))
        + power(float(ROWS - 1)) + power(float(ROWS - 2))
        + (jnp.broadcast_to(skip_gain[None, :], (8, 128)),),
        axis=0,
    )
    taps = jnp.concatenate([conv_taps.reshape(9, 128), jnp.zeros((7, 128), F32)], axis=0)
    og = jnp.concatenate([out_grad, jnp.zeros((128, 8), F32)], axis=1).T

    mine = after(mine, lam8, rho8, pwb, pwf, lam64, wt, consts, taps, og, at)
    other = to_chan(mine, 0, 0, 1)
    weight = in_weight.reshape(3, 8, 2, 256, 128)
    block, wblock = ((8, ROWS, 256), BF16), ((3, 8, 256, 128), BF16)
    half = far_call(
        half_kernel, 4.0, at, [((ROWS, 384), F32)], [block, wblock, ((ROWS, 384), F32)], 48, mine, weight
    )[0]
    given = lax.ppermute(mine, ("seq", "chan"), joint_pairs("give"))
    ext, prod, gl, st, send = call(
        states_kernel,
        8.0,
        at,
        [((528, 384), F32), ((ROWS, 128), F32), ((ROWS, 128), F32), ((64, 8, 128), F32), ((16, 48, 128), F32)],
        [block, wblock, ((64, 128), F32)],
        half, taps, og, lam8, pwf, pwb,
        far=(other, weight),
        sems=48,
        staged=True,
    )
    arrived = exchange(send, "seq")
    y, gp, sums = call(
        scan_kernel,
        7.0,
        None,
        [((SUB, 8, 128), F32)] * 2 + [((96, 8, 128), F32)],
        [],
        prod, gl, st, lam8, rho8, lam64,
    )
    shapes = [((8, ROWS, 256), BF16), ((8, 256, ROWS), BF16)]
    kept = far_call(turn_kernel, 3.5, at, shapes[1:], shapes, 16, mine, other, st)[0]
    given = after(given, arrived)
    passed = lax.ppermute(given, ("seq", "chan"), joint_pairs("pass"))
    mixed_out, low = call(
        grads_kernel,
        8.0,
        at,
        [((128, ROWS), F32), ((ROWS + 32, 384), BF16)],
        [((EXT, 128), F32), ((EXT, 128), F32), ((EXT, 384), F32), ((EXT, 384), F32)]
        + [((EXT, 128), F32), ((EXT, 128), F32), ((48, 128), F32)],
        arrived, wt, consts, lam8, rho8, pwf, pwb, y, gp, sums, st, ext, taps, og,
        late=(kept,),
        staged=True,
    )

    low_y = to_seq(low, 0, 1)
    low_core = to_chan(low, 0, 0, 1)
    terms = far_call(
        input_kernel,
        6.0,
        at,
        [((256, ROWS), BF16)] * 8,
        [((2, ROWS, 384), BF16), ((768, ROWS), BF16), ((8, 2, 3, 256, 128), BF16), ((8, 256, ROWS), BF16)],
        26,
        low, low_core, weight, partner.reshape(weight.shape),
    )
    grads = far_call(
        weight_kernel,
        5.0,
        at,
        [((8, 288, 384), BF16)],
        [((8, 256, ROWS), BF16), block, ((2, ROWS + 32, 384), BF16), ((8, 288, 384), BF16)],
        26,
        kept, given, passed, low, low_y, terms[0],
    )[0]
    terms = [terms[0]] + [to_chan(terms[r], r // 2, r % 2) for r in (2, 6, 4, 1, 3, 7, 5)]
    grads = exchange(grads, "seq", COLUMNS)
    input_grad = call(fold_input_kernel, 2.5, None, [((ROWS, 256), F32)], [], *terms)[0]
    weight_grad, small = call(
        fold_kernel, 2.5, None, [((3, 256, 128), F32), ((48, 128), F32)], [], grads
    )
    residue_grad = small[:32].reshape(2, MODES, 128)
    taps_grad = small[32:41].reshape(3, 3, 128)
    return (mixed_out, input_grad, weight_grad, taps_grad, residue_grad, small[41])


def solution(mesh):
    in_specs = (
        P("seq", "chan"),
        P(None, None, "chan"),
        P(None, None, "chan"),
        P(None, "chan"),
        P(None, "chan"),
        P(None, None, "chan"),
        P("chan"),
        P("chan", "seq"),
    )
    out_specs = (
        P("chan", "seq"),
        P("seq", "chan"),
        P(None, "seq", "chan"),
        P(None, None, "chan"),
        P(None, None, "chan"),
        P("chan"),
    )
    return jax.shard_map(
        on_device, mesh=mesh, in_specs=in_specs, out_specs=out_specs, check_vma=False
    )
```

```python
import jax
import jax.numpy as jnp
from jax import lax
from jax.experimental import pallas as pl
from jax.experimental.pallas import tpu as pltpu
from jax.sharding import PartitionSpec as P

F32 = jnp.float32
BF16 = jnp.bfloat16
MODES = 16
SUB = 64
ROWS = 8 * SUB
EXT = ROWS + 8


def chan_pairs(dx, dy, dc):
    pairs = []
    for c in range(16):
        x, y, core = c // 4, c // 2 % 2, c % 2
        pairs.append((c, (x + dx) % 4 * 4 + (y + dy) % 2 * 2 + (core + dc) % 2))
    return pairs


def seq_pairs(dz, dy):
    return [(s, (s // 2 + dz) % 8 * 2 + (s % 2 + dy) % 2) for s in range(16)]


def to_chan(x, dx, dy, dc=0):
    return lax.ppermute(x, "chan", chan_pairs(dx, dy, dc))


def to_seq(x, dz, dy=0):
    return lax.ppermute(x, "seq", seq_pairs(dz, dy))


def pole_power(rate, angle, count):
    high = jnp.round(angle * 1024.0) * (1.0 / 1024.0)
    low = angle - high
    one, two = high * count, low * count
    mag = jnp.exp(-rate * count)
    cos1, sin1, cos2, sin2 = jnp.cos(one), jnp.sin(one), jnp.cos(two), jnp.sin(two)
    return mag * (cos1 * cos2 - sin1 * sin2), mag * (sin1 * cos2 + cos1 * sin2)


COUNTS = (1.0, -1.0, float(ROWS), float(ROWS - 1), float(ROWS - 2), float(SUB), float(2 * SUB), float(4 * SUB))


def halves(ref, row=None):
    if row is None:
        return ref[0:MODES, :], ref[MODES : 2 * MODES, :]
    return ref[row, 0:MODES, :], ref[row, MODES : 2 * MODES, :]


def fill(pw, rows, dst):
    for n in range(2 * MODES):
        line = rows[n : n + 1, :] if pw is None else pw[rows, n : n + 1, :]
        dst[n] = jnp.broadcast_to(line, (8, 128))


def sub_powers(pw, dst, back):
    place = lax.broadcasted_iota(jnp.int32, (8, 128), 0)
    place = 7 - place if back else place
    for n in range(MODES):
        re, im = jnp.ones((8, 128), F32), jnp.zeros((8, 128), F32)
        for level in range(3):
            here = (place >> level) & 1 == 1
            step = pw[5 + level, n : n + 1, :], pw[5 + level, MODES + n : MODES + n + 1, :]
            step = tuple(jnp.where(here, s, t) for s, t in zip(step, (1.0, 0.0)))
            re, im = times((re, im), step)
        dst[n] = re
        dst[MODES + n] = im


def times(a, b):
    return a[0] * b[0] - a[1] * b[1], a[0] * b[1] + a[1] * b[0]


def copy_all(pairs, sems):
    copies = [pltpu.make_async_copy(a, b, sems.at[i]) for i, (a, b) in enumerate(pairs)]
    for c in copies:
        c.start()
    return copies


def wait_all(copies, start=False):
    for c in copies:
        if start:
            c.start()
        c.wait()


def stream(sources, weight_far, par, held, weight, sems):
    copies = []
    for b in range(8):
        pairs = [(weight_far.at[:, b, par], weight.at[:, b])]
        pairs += [(src.at[b], dst.at[b]) for src, dst in zip(sources, held)]
        group = [pltpu.make_async_copy(f, t, sems.at[6 * b + i]) for i, (f, t) in enumerate(pairs)]
        for c in group:
            c.start()
        copies.append(group)
    return copies


def columns(weight, b):
    return jnp.concatenate([weight[k, b] for k in range(3)], axis=1)


def convolve(taps, ext, k):
    lanes = slice(128 * k, 128 * k + 128)
    total = taps[k, 0:1, :] * ext[8 : 8 + ROWS, lanes]
    total = total + taps[k, 1:2, :] * ext[7 : 7 + ROWS, lanes]
    return total + taps[k, 2:3, :] * ext[6 : 6 + ROWS, lanes]


def half_kernel(at, mine_far, weight_far, out, mine, weight, made, sems):
    copies = stream([mine_far], weight_far, at[0], [mine], weight, sems)
    for b in range(0, 8, 2):
        for i in range(b, b + 2):
            wait_all(copies[i])
        left = jnp.concatenate([mine[i] for i in range(b, b + 2)], axis=1)
        right = jnp.concatenate([columns(weight, i) for i in range(b, b + 2)], axis=0)
        total = jnp.dot(left, right, preferred_element_type=F32)
        made[...] = total if b == 0 else made[...] + total
    wait_all([pltpu.make_async_copy(made, out, sems.at[0])], start=True)


def states_kernel(
    at, other_far, weight_far, half, taps, og, pw,
    ext, prod, gl, st, send, other, weight, ends, lam, pwf, pwb, sems, io,
):
    seq = at[2]
    copies = stream([other_far], weight_far, 1 - at[0], [other], weight, sems)
    io.need(3)
    fill(pw, 0, lam)
    sub_powers(pw, pwf, True)
    sub_powers(pw, pwb, False)
    for b in range(0, 8, 2):
        for i in range(b, b + 2):
            wait_all(copies[i])
        left = jnp.concatenate([other[i] for i in range(b, b + 2)], axis=1)
        right = jnp.concatenate([columns(weight, i) for i in range(b, b + 2)], axis=0)
        total = jnp.dot(left, right, preferred_element_type=F32)
        if b == 0:
            io.need(0)
        ext[8:520, :] = (half[...] if b == 0 else ext[8:520, :]) + total
    ext[0:8, :] = jnp.zeros((8, 384), F32)
    ext[520:528, :] = jnp.zeros((8, 384), F32)
    io.done(0)
    io.need(1, 2)
    q, k, v = (convolve(taps, ext, i) for i in range(3))
    fresh = lax.broadcasted_iota(jnp.int32, (ROWS, 128), 0) >= 2
    prod[...] = jnp.where(fresh, k * v, 0.0)
    cot = og[...].T
    gl[...] = jnp.where(fresh, cot * q, 0.0)
    io.done(1, 2)
    edge = [k[0:2], v[0:2], q[0:2], cot[0:2]]
    edge += [ext[518:520, 128 * i : 128 * i + 128] for i in range(3)]
    edge = jnp.concatenate(edge + [jnp.zeros((2, 128), F32)], axis=0)
    half = MODES // 2
    for src, powers, back, base in ((prod, pwf, False, 0), (gl, pwb, True, 32)):
        for n0 in range(0, MODES, half):

            def body(step, carry, n0=n0, back=back, src=src):
                i = SUB - 1 - step if back else step
                v = src[pl.ds(i, 8, stride=SUB), :]
                out = []
                for k in range(half):
                    re, im = carry[2 * k], carry[2 * k + 1]
                    lr, li = lam[n0 + k], lam[MODES + n0 + k]
                    out += [re * lr - im * li + v, re * li + im * lr]
                return tuple(out)

            zero = tuple(jnp.zeros((8, 128), F32) for _ in range(2 * half))
            carry = lax.fori_loop(0, SUB, body, zero, unroll=4)
            for k in range(half):
                n = n0 + k
                re, im = carry[2 * k], carry[2 * k + 1]
                st[base + n] = re
                st[base + MODES + n] = im
                er, ei = times((re, im), (powers[n], powers[MODES + n]))
                ends[base + n : base + n + 1, :] = jnp.sum(er, axis=0, keepdims=True)
                ends[base + MODES + n : base + MODES + n + 1, :] = jnp.sum(ei, axis=0, keepdims=True)
    io.done(3)
    for j in range(16):
        send[j, 0:32, :] = jnp.where(j >= seq, ends[0:32, :], ends[32:64, :])
        send[j, 32:48, :] = edge


def scan_kernel(prod, gl, st, pw, res, y, gp, sums, lam, rho):
    fill(pw, 0, lam)
    fill(None, res, rho)
    half = MODES // 2
    place = lax.broadcasted_iota(jnp.int32, (8, 128), 0)
    for base, back in ((0, False), (32, True)):
        for n in range(MODES):

            def shift(v, by, back=back):
                moved = pltpu.roll(v, 8 - by if back else by, 0)
                return jnp.where(place < 8 - by if back else place >= by, moved, 0.0)

            re, im = shift(st[base + n], 1), shift(st[base + MODES + n], 1)
            for level, by in enumerate((1, 2, 4)):
                ar, ai = times(
                    (shift(re, by), shift(im, by)),
                    (pw[5 + level, n : n + 1, :], pw[5 + level, MODES + n : MODES + n + 1, :]),
                )
                re, im = re + ar, im + ai
            sums[32 + base + n] = re
            sums[32 + base + MODES + n] = im
    for n0 in range(0, MODES, half):

        def forward(step, carry, n0=n0):
            p = prod[pl.ds(step, 8, stride=SUB), :]
            g = gl[pl.ds(step, 8, stride=SUB), :]
            out = []
            total = None
            for k in range(half):
                re, im, sr, si = carry[4 * k : 4 * k + 4]
                lr, li = lam[n0 + k], lam[MODES + n0 + k]
                re, im = re * lr - im * li + p, re * li + im * lr
                term = re * rho[n0 + k] - im * rho[MODES + n0 + k]
                total = term if total is None else total + term
                out += [re, im, sr + g * re, si + g * im]
            y[step] = total if n0 == 0 else y[step] + total
            return tuple(out)

        zero = tuple(jnp.zeros((8, 128), F32) for _ in range(4 * half))
        carry = lax.fori_loop(0, SUB, forward, zero, unroll=4)
        for k in range(half):
            sums[n0 + k] = carry[4 * k + 2]
            sums[MODES + n0 + k] = carry[4 * k + 3]

        def backward(step, carry, n0=n0):
            i = SUB - 1 - step
            g = gl[pl.ds(i, 8, stride=SUB), :]
            out = []
            total = None
            for k in range(half):
                re, im = carry[2 * k : 2 * k + 2]
                lr, li = lam[n0 + k], lam[MODES + n0 + k]
                re, im = re * lr - im * li + g, re * li + im * lr
                term = re * rho[n0 + k] - im * rho[MODES + n0 + k]
                total = term if total is None else total + term
                out += [re, im]
            gp[i] = total if n0 == 0 else gp[i] + total
            return tuple(out)

        zero = tuple(jnp.zeros((8, 128), F32) for _ in range(2 * half))
        lax.fori_loop(0, SUB, backward, zero, unroll=4)


def grads_kernel(
    at, arrived, pw, res, skip, y, gp, sums, st, ext, taps, og_far,
    mixed, low, yt, gt, gb, br, prod, gl, small, og, lam, rho, pwf, pwb, io,
):
    seq = at[2]

    io.need(1, 2, 9)
    fill(pw, 0, lam)
    fill(None, res, rho)
    sub_powers(pw, pwf, True)
    sub_powers(pw, pwb, False)
    lam16, inv16, lam512, lam511, lam510 = (halves(pw, i) for i in range(5))
    rho16 = halves(res)
    io.need(0, 3)
    zero16 = jnp.zeros((MODES, 128), F32)
    s_in, u_in = (zero16, zero16), (zero16, zero16)
    zero2 = jnp.zeros((2, 128), F32)
    own = nxt = [zero2] * 6
    rim = [zero2] * 3
    first = lax.broadcasted_iota(jnp.int32, (2, 128), 0) == 0

    def choose(flag, new, old):
        return [jnp.where(flag, a, b) for a, b in zip(new, old)]

    before = [zero2] * 3
    for j in range(16):
        tilde = arrived[j, 32:40, :]
        kvq = []
        for k, rows in ((1, tilde[0:2]), (2, tilde[2:4]), (0, tilde[4:6])):
            t1, t2 = taps[k, 1:2, :], taps[k, 2:3, :]
            p2, p1 = before[k][0:1], before[k][1:2]
            kvq.append(rows + jnp.where(first, t1 * p1 + t2 * p2, t2 * p1))
        out_grad = tilde[6:8]
        product = kvq[0] * kvq[1]
        cotangent = out_grad * kvq[2]
        mine = kvq + [out_grad, product, cotangent]
        tail = arrived[j, 40:48, :]
        before = [tail[0:2], tail[2:4], tail[4:6]]
        own = choose(j == seq, mine, own)
        nxt = choose(j == seq + 1, mine, nxt)
        rim = choose(j == seq - 1, before, rim)
        got = halves(arrived, j)
        p0, p1 = product[0:1], product[1:2]
        g0, g1 = cotangent[0:1], cotangent[1:2]
        ahead = j < seq
        fixed = [
            got[i] + jnp.where(ahead, lam511[i] * p0 + lam510[i] * p1, lam16[i] * g1 + (g0 if i == 0 else 0.0))
            for i in range(2)
        ]
        re, im = times(fixed, halves(pw, 8 + j))
        behind = j > seq
        s_in = (s_in[0] + jnp.where(ahead, re, 0.0), s_in[1] + jnp.where(ahead, im, 0.0))
        u_in = (u_in[0] + jnp.where(behind, re, 0.0), u_in[1] + jnp.where(behind, im, 0.0))

    def read_out(state):
        return jnp.sum(rho16[0] * state[0] - rho16[1] * state[1], axis=0, keepdims=True)

    p0, p1, g0, g1 = own[4][0:1], own[4][1:2], own[5][0:1], own[5][1:2]
    x0 = times(lam16, s_in)
    x0 = (x0[0] + p0, x0[1])
    x1 = times(lam16, x0)
    x1 = (x1[0] + p1, x1[1])
    small[0:16, :] = g0 * x0[0] + g1 * x1[0]
    small[16:32, :] = -(g0 * x0[1] + g1 * x1[1])
    inv2 = times(inv16, inv16)
    s_in = tuple(s_in[i] + inv16[i] * p0 + inv2[i] * p1 for i in range(2))
    carried = times(lam512, s_in)
    last = halves(arrived, seq)
    last = (last[0] + carried[0], last[1] + carried[1])
    for extra in range(2):
        moved = times(lam16, last)
        last = (moved[0] + nxt[4][extra : extra + 1], moved[1])
        yt[ROWS + extra : ROWS + extra + 1, :] = read_out(last)
    gt[ROWS : ROWS + 1, :] = read_out(u_in)
    later = times(inv16, (u_in[0] - nxt[5][0:1], u_in[1]))
    gt[ROWS + 1 : ROWS + 2, :] = read_out(later)
    yt[ROWS + 2 : EXT, :] = jnp.zeros((EXT - ROWS - 2, 128), F32)
    gt[ROWS + 2 : EXT, :] = jnp.zeros((EXT - ROWS - 2, 128), F32)
    io.need(4, 5, 6, 7)

    half = MODES // 2
    for n0 in range(0, MODES, half):
        start_f, start_b = [], []
        for k in range(half):
            n = n0 + k
            l8 = (lam[n], lam[MODES + n])
            r8 = (rho[n], rho[MODES + n])

            def full(state, powers, base, n=n):
                wide = tuple(jnp.broadcast_to(s[n : n + 1, :], (8, 128)) for s in state)
                add = times(wide, (powers[n], powers[MODES + n]))
                return times((sums[base + n] + add[0], sums[base + MODES + n] + add[1]), l8)

            q = full(s_in, pwb, 32)
            rr, ri = times(q, (st[32 + n], st[48 + n]))
            small[n : n + 1, :] += jnp.sum(sums[n] + rr, axis=0, keepdims=True)
            small[MODES + n : MODES + n + 1, :] -= jnp.sum(sums[MODES + n] + ri, axis=0, keepdims=True)
            start_f += list(times(q, r8))
            start_b += list(times(full(u_in, pwf, 64), r8))

        def follow(src, dst, back, start, n0=n0):
            def body(step, carry):
                i = SUB - 1 - step if back else step
                at = pl.ds(i, 8, stride=SUB)
                total = src[i] if n0 == 0 else dst[at, :]
                out = []
                for k in range(half):
                    re, im = carry[2 * k], carry[2 * k + 1]
                    total = total + re
                    lr, li = lam[n0 + k], lam[MODES + n0 + k]
                    out += [re * lr - im * li, re * li + im * lr]
                dst[at, :] = total
                return tuple(out)

            lax.fori_loop(0, SUB, body, tuple(start), unroll=4)

        follow(y, yt, False, start_f)
        follow(gp, gt, True, start_b)

    none, one = (jnp.ones_like(zero16), zero16), lam16
    yt[0:1, :] -= read_out(inv16) * p1
    gt[0:1, :] += read_out(none) * g0 + read_out(one) * g1
    gt[1:2, :] += read_out(none) * g1

    io.need(8, 10)
    og[0:ROWS, :] = og_far[...].T
    og[ROWS + 2 : EXT, :] = jnp.zeros((EXT - ROWS - 2, 128), F32)
    for k in range(3):
        ext[6:8, 128 * k : 128 * k + 128] = rim[k]
    og[ROWS : ROWS + 2, :] = nxt[3]
    for k, at_k in ((0, 2), (1, 0), (2, 1)):
        lanes = slice(128 * k, 128 * k + 128)
        br[0:ROWS, lanes] = convolve(taps, ext, k)
        br[ROWS : ROWS + 2, lanes] = nxt[at_k]
    br[ROWS + 2 : EXT, :] = jnp.zeros((EXT - ROWS - 2, 384), F32)
    prod[...] = br[:, 128:256] * br[:, 256:384]
    gl[...] = og[...] * br[:, 0:128]
    gain = skip[...]
    long_out = yt[...] + gain * prod[...]
    gb[:, 0:128] = og[...] * long_out
    grad_prod = gt[...] + gain * gl[...]
    gb[:, 128:256] = grad_prod * br[:, 256:384]
    gb[:, 256:384] = grad_prod * br[:, 128:256]
    for k in range(3):
        lanes = slice(128 * k, 128 * k + 128)
        total = None
        for j in range(3):
            term = taps[k, j : j + 1, :] * gb[j : j + ROWS, lanes]
            total = term if total is None else total + term
            row = 32 + 3 * k + j
            small[row : row + 1, :] = jnp.sum(
                gb[0:ROWS, lanes] * ext[8 - j : 8 - j + ROWS, lanes], axis=0, keepdims=True
            )
        low[0:ROWS, lanes] = total.astype(BF16)
    small[41:42, :] = jnp.sum(gl[0:ROWS, :] * prod[0:ROWS, :], axis=0, keepdims=True)
    small[42:48, :] = jnp.zeros((6, 128), F32)
    wide = jnp.concatenate([small[16 * i : 16 * i + 16, :] for i in range(3)], axis=1)
    split_rows(wide, low, ROWS)
    io.done(1)
    mixed[...] = (br[0:ROWS, 0:128] * long_out[0:ROWS, :]).T


def split_rows(wide, dst, row):
    high = wide.astype(BF16)
    dst[row : row + 16, :] = high
    dst[row + 16 : row + 32, :] = (wide - high.astype(F32)).astype(BF16)


def join_rows(src, row):
    return src[row : row + 16, :].astype(F32) + src[row + 16 : row + 32, :].astype(F32)


def input_kernel(at, low, low_core, weight, partner, out, left, lturn, right, parts, sems):
    core = at[0]
    copies = copy_all([(low.at[0:ROWS], left.at[0]), (low_core.at[0:ROWS], left.at[1])], sems)
    far = []
    for n in range(8):
        for s, src in enumerate((weight, partner)):
            c = pltpu.make_async_copy(src.at[:, n, core], right.at[n, s], sems.at[2 + 2 * n + s])
            c.start()
            far.append(c)
    wait_all(copies)
    lturn[...] = jnp.concatenate([left[0].T, left[1].T], axis=0)
    sent = []
    for n in range(0, 8, 2):
        wait_all(far[2 * n : 2 * n + 4])
        cols = [
            jnp.concatenate([right[i, s, k] for s in range(2) for k in range(3)], axis=1)
            for i in (n, n + 1)
        ]
        cols = jnp.concatenate(cols, axis=0)
        total = jnp.dot(cols, lturn[...], preferred_element_type=F32).astype(BF16)
        for i in range(2):
            parts[n + i] = total[256 * i : 256 * i + 256]
            c = pltpu.make_async_copy(parts.at[n + i], out.at[n + i], sems.at[18 + n + i])
            c.start()
            sent.append(c)
    wait_all(sent)


FAR_ORDER = (4, 3, -3, 1, -1, 2, -2, 0)
HALF = 128


def weight_kernel(at, mine, other, given, passed, low, low_y, _, *rest):
    outs, (held, cols, made, far_made, near_made, sems) = rest[:7], rest[7:]
    z = at[6]
    one, one_back, four, four_back, near, middle, own_small = outs
    far = []
    for n, d in enumerate(FAR_ORDER):
        p = lax.rem(z + (d + 8), 8)
        for s, pair in enumerate(((other, mine), (passed, given))):
            dst = held.at[n, ROWS * s : ROWS * s + ROWS]
            for flag, src in enumerate(pair):
                c = pltpu.make_async_copy(src.at[p], dst, sems.at[2 + 2 * n + s])

                @pl.when(at[3] == flag)
                def _(c=c):
                    c.start()

            far.append(c)
        if n == 0:
            copies = copy_all([(low, cols.at[0]), (low_y, cols.at[1])], sems)
    wait_all(copies)
    right = jnp.concatenate([cols[0, 0:ROWS, :], cols[1, 0:ROWS, :]], axis=0)
    wide = join_rows(cols.at[0], ROWS) + join_rows(cols.at[1], ROWS)
    for i in range(2):
        split_rows(wide, made.at[i], 512)
        split_rows(wide, far_made.at[i], HALF)
    sent = []

    def send(src, dst):
        c = pltpu.make_async_copy(src, dst, sems.at[18 + len(sent)])
        c.start()
        sent.append(c)

    send(made.at[0, 512:544], own_small)
    for n, d in enumerate(FAR_ORDER):
        if n % 2 == 0:
            wait_all(far[2 * n : 2 * n + 4])
            both = jnp.concatenate([held[n], held[n + 1]], axis=1)
            both = lax.dot_general(both, right, (((0,), (0,)), ((), ())), preferred_element_type=F32)
        total = both[256 * (n % 2) : 256 * (n % 2) + 256]
        if n == 0:
            total = total.astype(BF16)
            far_made[0, 0:HALF, :] = total[HALF:]
            far_made[1, 0:HALF, :] = total[0:HALF]
            send(far_made.at[0], four)
            send(far_made.at[1], four_back)
        elif n < 5:
            row = 0 if n < 3 else 256
            made[(n - 1) % 2, row : row + 256, :] = total.astype(BF16)
            if n >= 3:
                send(made.at[n - 3], (one, one_back)[n - 3])
        else:
            near_made[n - 5] = total
            send(near_made.at[n - 5], middle if n == 7 else near.at[n - 5])
    wait_all(sent)


def relay_kernel(near, one, four, one_back, four_back, back, ahead, io):
    io.need(0, 3, 4)
    total = near[1] + one_back[0:256, :].astype(F32)
    back[0:HALF, :] = (total[0:HALF] + four_back[0:HALF, :].astype(F32)).astype(BF16)
    back[HALF:256, :] = total[HALF:].astype(BF16)
    back[256:288, :] = one_back[512:544, :]
    back[288:320, :] = four_back[HALF : HALF + 32, :]
    io.done(0)
    io.need(1, 2)
    total = near[0] + one[0:256, :].astype(F32)
    ahead[0:HALF, :] = total[0:HALF].astype(BF16)
    ahead[HALF:256, :] = (total[HALF:] + four[0:HALF, :].astype(F32)).astype(BF16)
    ahead[256:288, :] = one[512:544, :]


def fold_input_kernel(parts, out):
    total = parts[0].astype(F32)
    for j in range(1, 8):
        total = total + parts[j].astype(F32)
    out[...] = total.T


def early_kernel(middle, one, one_back, out):
    out[...] = middle[...] + one[256:512, :].astype(F32) + one_back[256:512, :].astype(F32)


def fold_kernel(
    at, early, back, ahead, own_small, one, one_back, four, four_back, out, res, taps, skip, table, io
):
    z = at[6]
    io.need(0, 1, 2)
    total = early[...] + back[0:256, :].astype(F32) + ahead[0:256, :].astype(F32)
    for k in range(3):
        out[k] = total[:, 128 * k : 128 * k + 128]
    io.done(0)
    io.need(3, 4, 5, 6, 7)
    came = ((own_small, 0, 0), (one, 0, -1), (four, 0, -2), (ahead, 256, -3))
    came += ((one_back, 0, 1), (four_back, 0, 2), (back, 256, 3), (back, 288, 4))
    for src, row, d in came:
        table[lax.rem(z + (d + 8), 8)] = join_rows(src, row)
    wide = table[0]
    for j in range(1, 8):
        wide = wide + table[j]
    res[0] = wide[:, 0:128]
    res[1] = wide[:, 128:256]
    for k in range(3):
        taps[k] = wide[3 * k : 3 * k + 3, 256:384]
    skip[...] = wide[9:10, 256:384]


VMEM_BYTES = 64 * 1024 * 1024 - 128 * 1024
FAR = pl.BlockSpec(memory_space=pltpu.HBM)
SCALARS = pl.BlockSpec(memory_space=pltpu.SMEM)


def raw_call(kernel, us, outs, scratch, sems, args, in_specs, out_specs):
    return pl.pallas_call(
        kernel,
        in_specs=in_specs,
        out_specs=out_specs,
        out_shape=[jax.ShapeDtypeStruct(s, t) for s, t in outs],
        scratch_shapes=[pltpu.VMEM(s, t) for s, t in scratch] + [pltpu.SemaphoreType.DMA((sems,))],
        compiler_params=pltpu.CompilerParams(vmem_limit_bytes=VMEM_BYTES),
        cost_estimate=pl.CostEstimate(flops=int(us * 1.1e9), bytes_accessed=0, transcendentals=0),
    )(*args)


def far_call(kernel, us, at, outs, scratch, sems, *args):
    scalars = () if at is None else (at,)
    specs = [SCALARS] * len(scalars) + [FAR] * len(args)
    return raw_call(kernel, us, outs, scratch, sems, scalars + args, specs, [FAR] * len(outs))


class Staged:
    def __init__(self, ins, outs):
        self.ins, self.outs, self.here, self.gone = ins, outs, set(), set()

    def need(self, *which):
        for i in which:
            if i not in self.here:
                self.here.add(i)
                self.ins[i].wait()

    def done(self, *which):
        for i in which:
            if i not in self.gone:
                self.gone.add(i)
                self.outs[i].start()


def call(kernel, us, at, outs, scratch, *args, far=(), sems=0, late=(), staged=False, windows=()):
    scalars = () if at is None else (at,)
    n_s, n_f, n_i, n_l, n_o = len(scalars), len(far), len(args), len(late), len(outs)

    def body(*refs):
        refs = list(refs)

        def take(count):
            head = refs[:count]
            del refs[:count]
            return head

        top, far_refs, ins, _, results = take(n_s), take(n_f), take(n_i), take(n_l), take(n_o)
        held, made, own, sem = take(n_i), take(n_o), refs[:-1], refs[-1]

        def copies(pairs, base):
            return [pltpu.make_async_copy(a, b, sem.at[base + i]) for i, (a, b) in enumerate(pairs)]

        for i, row in windows:
            ins[i] = ins[i].at[row : row + 32]
        coming = copies(zip(ins, held), sems)
        for c in coming:
            c.start()
        io = Staged(coming, copies(zip(made, results), sems + n_i))
        if not staged:
            io.need(*range(n_i))
        extra = ((sem,) if far else ()) + ((io,) if staged else ())
        kernel(*top, *far_refs, *held, *made, *own, *extra)
        io.need(*range(n_i))
        io.done(*range(n_o))
        wait_all(io.outs)

    shapes = [(a.shape, a.dtype) for a in args]
    for i, _ in windows:
        shapes[i] = ((32, args[i].shape[1]), args[i].dtype)
    buffers = shapes + list(outs) + list(scratch)
    specs = [SCALARS] * n_s + [FAR] * (n_f + n_i + n_l)
    total = sems + n_i + n_o
    return raw_call(
        body, us, outs, buffers, total, scalars + tuple(far) + args + tuple(late), specs, [FAR] * n_o
    )


def after(x, *deps):
    return pl.pallas_call(
        lambda *_: None,
        in_specs=[pl.BlockSpec(memory_space=pl.ANY)] * (1 + len(deps)),
        out_specs=pl.BlockSpec(memory_space=pl.ANY),
        out_shape=jax.ShapeDtypeStruct(x.shape, x.dtype),
        input_output_aliases={0: 0},
    )(x, *deps)


CHIPS = [[x * 4 + y * 2 + c for x in range(4) for y in range(2)] for c in range(2)]
COLUMNS = [[z * 2 + y for z in range(8)] for y in range(2)]


def exchange(x, axis, groups=None):
    return lax.all_to_all(
        x, axis, split_axis=0, concat_axis=0, tiled=True, axis_index_groups=groups
    )


def joint_pairs(kind):
    pairs = []
    for s in range(16):
        for c in range(16):
            wanted = s % 2 == c % 2
            if kind == "give" and not wanted:
                pairs.append((s * 16 + c, (s ^ 1) * 16 + c))
            if kind == "pass" and wanted:
                pairs.append((s * 16 + c, s * 16 + (c ^ 1)))
    return pairs


def on_device(
    hidden_in, in_weight, conv_taps, decay_rate, mode_angle, residue, skip_gain, out_grad
):
    chan, seq = lax.axis_index("chan"), lax.axis_index("seq")
    core, yl = chan % 2, seq % 2
    same = (yl == core).astype(jnp.int32)
    at = jnp.stack([core, chan, seq, same, chan // 4, chan // 2 % 2, seq // 2]).astype(jnp.int32)

    mine = exchange(jnp.broadcast_to(hidden_in[None], (8, ROWS, 256)), "chan", CHIPS)
    partner = to_chan(in_weight, 0, 0, 1)

    away = jnp.abs(jnp.arange(16, dtype=jnp.int32) - seq).astype(F32) - 1.0
    counts = jnp.concatenate([jnp.array(COUNTS, F32), jnp.maximum(away, 0.0) * float(ROWS)])
    pw = pole_power(decay_rate[None], mode_angle[None], counts[:, None, None])
    pw = jnp.concatenate(pw, axis=1)
    res = residue.reshape(2 * MODES, 128)

    mine = after(mine, pw, at)
    other = to_chan(mine, 0, 0, 1)
    weight = in_weight.reshape(3, 8, 2, 256, 128)
    block, wblock = ((8, ROWS, 256), BF16), ((3, 8, 256, 128), BF16)
    half = far_call(
        half_kernel, 4.0, at, [((ROWS, 384), F32)], [block, wblock, ((ROWS, 384), F32)], 48, mine, weight
    )[0]
    given = lax.ppermute(mine, ("seq", "chan"), joint_pairs("give"))
    ext, prod, gl, st, send = call(
        states_kernel,
        8.0,
        at,
        [((528, 384), F32), ((ROWS, 128), F32), ((ROWS, 128), F32), ((64, 8, 128), F32), ((16, 48, 128), F32)],
        [block, wblock, ((64, 128), F32)] + [((32, 8, 128), F32)] * 3,
        half, conv_taps, out_grad, pw,
        far=(other, weight),
        sems=48,
        staged=True,
    )
    arrived = exchange(send, "seq")
    y, gp, sums = call(
        scan_kernel,
        7.0,
        None,
        [((SUB, 8, 128), F32)] * 2 + [((96, 8, 128), F32)],
        [((32, 8, 128), F32)] * 2,
        prod, gl, st, pw, res,
    )
    given = after(given, arrived, y)
    passed = lax.ppermute(given, ("seq", "chan"), joint_pairs("pass"))
    mixed_out, low = call(
        grads_kernel,
        8.0,
        at,
        [((128, ROWS), F32), ((ROWS + 32, 384), BF16)],
        [((EXT, 128), F32), ((EXT, 128), F32), ((EXT, 384), F32), ((EXT, 384), F32)]
        + [((EXT, 128), F32), ((EXT, 128), F32), ((48, 128), F32), ((EXT, 128), F32)]
        + [((32, 8, 128), F32)] * 4,
        arrived, pw, res, skip_gain[None, :], y, gp, sums, st, ext, conv_taps, out_grad,
        staged=True,
    )

    low_y = to_seq(low, 0, 1)
    low_core = to_chan(low, 0, 0, 1)
    terms = far_call(
        input_kernel,
        6.0,
        at,
        [((8, 256, ROWS), BF16)],
        [((2, ROWS, 384), BF16), ((768, ROWS), BF16), ((8, 2, 3, 256, 128), BF16), ((8, 256, ROWS), BF16)],
        26,
        low, low_core, weight, partner.reshape(weight.shape),
    )[0]
    pair_rows, half_rows = ((544, 384), BF16), ((HALF + 32, 384), BF16)
    one, one_back, four, four_back, near, middle, own_small = far_call(
        weight_kernel,
        40.0,
        at,
        [pair_rows] * 2 + [half_rows] * 2
        + [((2, 256, 384), F32), ((256, 384), F32), ((32, 384), BF16)],
        [((8, 2 * ROWS, 256), BF16), ((2, ROWS + 32, 384), BF16), ((2, 544, 384), BF16)]
        + [((2, HALF + 32, 384), BF16), ((3, 256, 384), F32)],
        28,
        mine, other, given, passed, low, low_y, terms,
    )
    terms = exchange(terms, "chan", CHIPS)
    four, four_back = to_seq(four, 2), to_seq(four_back, -2)
    one, one_back = to_seq(one, 1), to_seq(one_back, -1)
    back, ahead = call(
        relay_kernel,
        2.0,
        None,
        [((320, 384), BF16), ((288, 384), BF16)],
        [],
        near, one, four, one_back, four_back,
        staged=True,
    )
    back, ahead = to_seq(back, -2), to_seq(ahead, 2)
    input_grad = call(fold_input_kernel, 2.5, None, [((ROWS, 256), F32)], [], terms)[0]
    early = call(early_kernel, 2.0, None, [((256, 384), F32)], [], middle, one, one_back)[0]
    weight_grad, residue_grad, taps_grad, skip_grad = call(
        fold_kernel,
        2.5,
        at,
        [((3, 256, 128), F32), ((2, MODES, 128), F32), ((3, 3, 128), F32), ((1, 128), F32)],
        [((8, 16, 384), F32)],
        early, back, ahead, own_small, one, one_back, four, four_back,
        windows=((4, 512), (5, 512), (6, HALF), (7, HALF)),
        late=(input_grad,),
        staged=True,
    )
    return (mixed_out, input_grad, weight_grad, taps_grad, residue_grad, skip_grad.reshape(128))


def solution(mesh):
    in_specs = (
        P("seq", "chan"),
        P(None, None, "chan"),
        P(None, None, "chan"),
        P(None, "chan"),
        P(None, "chan"),
        P(None, None, "chan"),
        P("chan"),
        P("chan", "seq"),
    )
    out_specs = (
        P("chan", "seq"),
        P("seq", "chan"),
        P(None, "seq", "chan"),
        P(None, None, "chan"),
        P(None, None, "chan"),
        P("chan"),
    )
    return jax.shard_map(
        on_device, mesh=mesh, in_specs=in_specs, out_specs=out_specs, check_vma=False
    )
```

```python
import jax
import jax.numpy as jnp
from jax import lax
from jax.experimental import pallas as pl
from jax.experimental.pallas import tpu as pltpu
from jax.sharding import PartitionSpec as P

F32 = jnp.float32
BF16 = jnp.bfloat16
MODES = 16
SUB = 64
ROWS = 8 * SUB
EXT = ROWS + 8
SPAN = ROWS + SUB


def chan_pairs(dx, dy, dc):
    pairs = []
    for c in range(16):
        x, y, core = c // 4, c // 2 % 2, c % 2
        pairs.append((c, (x + dx) % 4 * 4 + (y + dy) % 2 * 2 + (core + dc) % 2))
    return pairs


def seq_pairs(dz, dy):
    return [(s, (s // 2 + dz) % 8 * 2 + (s % 2 + dy) % 2) for s in range(16)]


def to_chan(x, dx, dy, dc=0):
    return lax.ppermute(x, "chan", chan_pairs(dx, dy, dc))


def to_seq(x, dz, dy=0):
    return lax.ppermute(x, "seq", seq_pairs(dz, dy))


def pole_power(rate, angle, count):
    high = jnp.round(angle * 1024.0) * (1.0 / 1024.0)
    low = angle - high
    one, two = high * count, low * count
    mag = jnp.exp(-rate * count)
    cos1, sin1, cos2, sin2 = jnp.cos(one), jnp.sin(one), jnp.cos(two), jnp.sin(two)
    return mag * (cos1 * cos2 - sin1 * sin2), mag * (sin1 * cos2 + cos1 * sin2)


COUNTS = (1.0, -1.0, float(ROWS), float(ROWS - 1), float(ROWS - 2), float(SUB), float(2 * SUB), float(4 * SUB))


def halves(ref, row=None):
    if row is None:
        return ref[0:MODES, :], ref[MODES : 2 * MODES, :]
    return ref[row, 0:MODES, :], ref[row, MODES : 2 * MODES, :]


def fill(pw, rows, dst):
    for n in range(2 * MODES):
        line = rows[n : n + 1, :] if pw is None else pw[rows, n : n + 1, :]
        dst[n] = jnp.broadcast_to(line, (8, 128))


def sub_powers(pw, dst, back):
    place = lax.broadcasted_iota(jnp.int32, (8, 128), 0)
    place = 7 - place if back else place
    for n in range(MODES):
        re, im = jnp.ones((8, 128), F32), jnp.zeros((8, 128), F32)
        for level in range(3):
            here = (place >> level) & 1 == 1
            step = pw[5 + level, n : n + 1, :], pw[5 + level, MODES + n : MODES + n + 1, :]
            step = tuple(jnp.where(here, s, t) for s, t in zip(step, (1.0, 0.0)))
            re, im = times((re, im), step)
        dst[n] = re
        dst[MODES + n] = im


def times(a, b):
    return a[0] * b[0] - a[1] * b[1], a[0] * b[1] + a[1] * b[0]


def copy_all(pairs, sems):
    copies = [pltpu.make_async_copy(a, b, sems.at[i]) for i, (a, b) in enumerate(pairs)]
    for c in copies:
        c.start()
    return copies


def wait_all(copies, start=False):
    for c in copies:
        if start:
            c.start()
        c.wait()


def stream(sources, weight_far, par, held, weight, sems):
    copies = []
    for b in range(8):
        pairs = [(weight_far.at[:, b, par], weight.at[:, b])]
        pairs += [(src.at[b], dst.at[b]) for src, dst in zip(sources, held)]
        group = [pltpu.make_async_copy(f, t, sems.at[6 * b + i]) for i, (f, t) in enumerate(pairs)]
        for c in group:
            c.start()
        copies.append(group)
    return copies


def columns(weight, b):
    return jnp.concatenate([weight[k, b] for k in range(3)], axis=1)


def convolve(taps, ext, k):
    lanes = slice(128 * k, 128 * k + 128)
    total = taps[k, 0:1, :] * ext[8 : 8 + ROWS, lanes]
    total = total + taps[k, 1:2, :] * ext[7 : 7 + ROWS, lanes]
    return total + taps[k, 2:3, :] * ext[6 : 6 + ROWS, lanes]


def half_kernel(at, mine_far, weight_far, out, mine, weight, made, sems):
    copies = stream([mine_far], weight_far, at[0], [mine], weight, sems)
    for b in range(0, 8, 2):
        for i in range(b, b + 2):
            wait_all(copies[i])
        left = jnp.concatenate([mine[i] for i in range(b, b + 2)], axis=1)
        right = jnp.concatenate([columns(weight, i) for i in range(b, b + 2)], axis=0)
        total = jnp.dot(left, right, preferred_element_type=F32)
        made[...] = total if b == 0 else made[...] + total
    wait_all([pltpu.make_async_copy(made, out, sems.at[0])], start=True)


def states_kernel(
    at, other_far, weight_far, half, taps, og, pw,
    ext, prod, gl, st, send, other, weight, ends, lam, pwf, pwb, sems, io,
):
    seq = at[2]
    copies = stream([other_far], weight_far, 1 - at[0], [other], weight, sems)
    io.need(3)
    fill(pw, 0, lam)
    sub_powers(pw, pwf, True)
    sub_powers(pw, pwb, False)
    for b in range(0, 8, 2):
        for i in range(b, b + 2):
            wait_all(copies[i])
        left = jnp.concatenate([other[i] for i in range(b, b + 2)], axis=1)
        right = jnp.concatenate([columns(weight, i) for i in range(b, b + 2)], axis=0)
        total = jnp.dot(left, right, preferred_element_type=F32)
        if b == 0:
            io.need(0)
        ext[8:520, :] = (half[...] if b == 0 else ext[8:520, :]) + total
    ext[0:8, :] = jnp.zeros((8, 384), F32)
    ext[520:528, :] = jnp.zeros((8, 384), F32)
    io.done(0)
    io.need(1, 2)
    q, k, v = (convolve(taps, ext, i) for i in range(3))
    fresh = lax.broadcasted_iota(jnp.int32, (ROWS, 128), 0) >= 2
    prod[0:ROWS, :] = jnp.where(fresh, k * v, 0.0)
    cot = og[...].T
    gl[0:ROWS, :] = jnp.where(fresh, cot * q, 0.0)
    io.done(1, 2)
    edge = [k[0:2], v[0:2], q[0:2], cot[0:2]]
    edge += [ext[518:520, 128 * i : 128 * i + 128] for i in range(3)]
    edge = jnp.concatenate(edge + [jnp.zeros((2, 128), F32)], axis=0)
    half = MODES // 2
    for src, powers, back, base in ((prod, pwf, False, 0), (gl, pwb, True, 32)):
        for n0 in range(0, MODES, half):

            def body(step, carry, n0=n0, back=back, src=src):
                i = SUB - 1 - step if back else step
                v = src[pl.ds(i, 8, stride=SUB), :]
                out = []
                for k in range(half):
                    re, im = carry[2 * k], carry[2 * k + 1]
                    lr, li = lam[n0 + k], lam[MODES + n0 + k]
                    out += [re * lr - im * li + v, re * li + im * lr]
                return tuple(out)

            zero = tuple(jnp.zeros((8, 128), F32) for _ in range(2 * half))
            carry = lax.fori_loop(0, SUB, body, zero, unroll=4)
            for k in range(half):
                n = n0 + k
                re, im = carry[2 * k], carry[2 * k + 1]
                st[base + n] = re
                st[base + MODES + n] = im
                er, ei = times((re, im), (powers[n], powers[MODES + n]))
                ends[base + n : base + n + 1, :] = jnp.sum(er, axis=0, keepdims=True)
                ends[base + MODES + n : base + MODES + n + 1, :] = jnp.sum(ei, axis=0, keepdims=True)
    io.done(3)
    for j in range(16):
        send[j, 0:32, :] = jnp.where(j >= seq, ends[0:32, :], ends[32:64, :])
        send[j, 32:48, :] = edge


def scan_kernel(prod, gl, st, pw, res, y, gp, sums, lam, rho):
    fill(pw, 0, lam)
    fill(None, res, rho)
    half = MODES // 2
    place = lax.broadcasted_iota(jnp.int32, (8, 128), 0)
    for base, back in ((0, False), (32, True)):
        for n in range(MODES):

            def shift(v, by, back=back):
                moved = pltpu.roll(v, 8 - by if back else by, 0)
                return jnp.where(place < 8 - by if back else place >= by, moved, 0.0)

            re, im = shift(st[base + n], 1), shift(st[base + MODES + n], 1)
            for level, by in enumerate((1, 2, 4)):
                ar, ai = times(
                    (shift(re, by), shift(im, by)),
                    (pw[5 + level, n : n + 1, :], pw[5 + level, MODES + n : MODES + n + 1, :]),
                )
                re, im = re + ar, im + ai
            sums[32 + base + n] = re
            sums[32 + base + MODES + n] = im
    for n0 in range(0, MODES, half):

        def forward(step, carry, n0=n0):
            p = prod[pl.ds(step, 8, stride=SUB), :]
            g = gl[pl.ds(step, 8, stride=SUB), :]
            out = []
            total = None
            for k in range(half):
                re, im, sr, si = carry[4 * k : 4 * k + 4]
                lr, li = lam[n0 + k], lam[MODES + n0 + k]
                re, im = re * lr - im * li + p, re * li + im * lr
                term = re * rho[n0 + k] - im * rho[MODES + n0 + k]
                total = term if total is None else total + term
                out += [re, im, sr + g * re, si + g * im]
            y[step] = total if n0 == 0 else y[step] + total
            return tuple(out)

        zero = tuple(jnp.zeros((8, 128), F32) for _ in range(4 * half))
        carry = lax.fori_loop(0, SUB, forward, zero, unroll=4)
        for k in range(half):
            sums[n0 + k] = carry[4 * k + 2]
            sums[MODES + n0 + k] = carry[4 * k + 3]

        def backward(step, carry, n0=n0):
            i = SUB - 1 - step
            g = gl[pl.ds(i, 8, stride=SUB), :]
            out = []
            total = None
            for k in range(half):
                re, im = carry[2 * k : 2 * k + 2]
                lr, li = lam[n0 + k], lam[MODES + n0 + k]
                re, im = re * lr - im * li + g, re * li + im * lr
                term = re * rho[n0 + k] - im * rho[MODES + n0 + k]
                total = term if total is None else total + term
                out += [re, im]
            gp[i] = total if n0 == 0 else gp[i] + total
            return tuple(out)

        zero = tuple(jnp.zeros((8, 128), F32) for _ in range(2 * half))
        lax.fori_loop(0, SUB, backward, zero, unroll=4)


def grads_kernel(
    at, arrived, pw, res, skip, y, gp, sums, st, ext, taps, og_far,
    mixed, low, yt, gt, gb, br, prod, gl, small, og, lam, rho, pwf, pwb, io,
):
    seq = at[2]

    io.need(1, 2, 9)
    fill(pw, 0, lam)
    fill(None, res, rho)
    sub_powers(pw, pwf, True)
    sub_powers(pw, pwb, False)
    lam16, inv16, lam512, lam511, lam510 = (halves(pw, i) for i in range(5))
    rho16 = halves(res)
    io.need(0, 3)
    zero16 = jnp.zeros((MODES, 128), F32)
    s_in, u_in = (zero16, zero16), (zero16, zero16)
    zero2 = jnp.zeros((2, 128), F32)
    own = nxt = [zero2] * 6
    rim = [zero2] * 3
    first = lax.broadcasted_iota(jnp.int32, (2, 128), 0) == 0

    def choose(flag, new, old):
        return [jnp.where(flag, a, b) for a, b in zip(new, old)]

    before = [zero2] * 3
    for j in range(16):
        tilde = arrived[j, 32:40, :]
        kvq = []
        for k, rows in ((1, tilde[0:2]), (2, tilde[2:4]), (0, tilde[4:6])):
            t1, t2 = taps[k, 1:2, :], taps[k, 2:3, :]
            p2, p1 = before[k][0:1], before[k][1:2]
            kvq.append(rows + jnp.where(first, t1 * p1 + t2 * p2, t2 * p1))
        out_grad = tilde[6:8]
        product = kvq[0] * kvq[1]
        cotangent = out_grad * kvq[2]
        mine = kvq + [out_grad, product, cotangent]
        tail = arrived[j, 40:48, :]
        before = [tail[0:2], tail[2:4], tail[4:6]]
        own = choose(j == seq, mine, own)
        nxt = choose(j == seq + 1, mine, nxt)
        rim = choose(j == seq - 1, before, rim)
        got = halves(arrived, j)
        p0, p1 = product[0:1], product[1:2]
        g0, g1 = cotangent[0:1], cotangent[1:2]
        ahead = j < seq
        fixed = [
            got[i] + jnp.where(ahead, lam511[i] * p0 + lam510[i] * p1, lam16[i] * g1 + (g0 if i == 0 else 0.0))
            for i in range(2)
        ]
        re, im = times(fixed, halves(pw, 8 + j))
        behind = j > seq
        s_in = (s_in[0] + jnp.where(ahead, re, 0.0), s_in[1] + jnp.where(ahead, im, 0.0))
        u_in = (u_in[0] + jnp.where(behind, re, 0.0), u_in[1] + jnp.where(behind, im, 0.0))

    def read_out(state):
        return jnp.sum(rho16[0] * state[0] - rho16[1] * state[1], axis=0, keepdims=True)

    p0, p1, g0, g1 = own[4][0:1], own[4][1:2], own[5][0:1], own[5][1:2]
    x0 = times(lam16, s_in)
    x0 = (x0[0] + p0, x0[1])
    x1 = times(lam16, x0)
    x1 = (x1[0] + p1, x1[1])
    small[0:16, :] = g0 * x0[0] + g1 * x1[0]
    small[16:32, :] = -(g0 * x0[1] + g1 * x1[1])
    inv2 = times(inv16, inv16)
    s_in = tuple(s_in[i] + inv16[i] * p0 + inv2[i] * p1 for i in range(2))
    carried = times(lam512, s_in)
    last = halves(arrived, seq)
    last = (last[0] + carried[0], last[1] + carried[1])
    for extra in range(2):
        moved = times(lam16, last)
        last = (moved[0] + nxt[4][extra : extra + 1], moved[1])
        yt[ROWS + extra : ROWS + extra + 1, :] = read_out(last)
    gt[ROWS : ROWS + 1, :] = read_out(u_in)
    later = times(inv16, (u_in[0] - nxt[5][0:1], u_in[1]))
    gt[ROWS + 1 : ROWS + 2, :] = read_out(later)
    yt[ROWS + 2 : EXT, :] = jnp.zeros((EXT - ROWS - 2, 128), F32)
    gt[ROWS + 2 : EXT, :] = jnp.zeros((EXT - ROWS - 2, 128), F32)
    io.need(4, 5, 6, 7)

    half = MODES // 2
    for n0 in range(0, MODES, half):
        start_f, start_b = [], []
        for k in range(half):
            n = n0 + k
            l8 = (lam[n], lam[MODES + n])
            r8 = (rho[n], rho[MODES + n])

            def full(state, powers, base, n=n):
                wide = tuple(jnp.broadcast_to(s[n : n + 1, :], (8, 128)) for s in state)
                add = times(wide, (powers[n], powers[MODES + n]))
                return times((sums[base + n] + add[0], sums[base + MODES + n] + add[1]), l8)

            q = full(s_in, pwb, 32)
            rr, ri = times(q, (st[32 + n], st[48 + n]))
            small[n : n + 1, :] += jnp.sum(sums[n] + rr, axis=0, keepdims=True)
            small[MODES + n : MODES + n + 1, :] -= jnp.sum(sums[MODES + n] + ri, axis=0, keepdims=True)
            start_f += list(times(q, r8))
            start_b += list(times(full(u_in, pwf, 64), r8))

        def follow(src, dst, back, start, n0=n0):
            def body(step, carry):
                i = SUB - 1 - step if back else step
                at = pl.ds(i, 8, stride=SUB)
                total = src[i] if n0 == 0 else dst[at, :]
                out = []
                for k in range(half):
                    re, im = carry[2 * k], carry[2 * k + 1]
                    total = total + re
                    lr, li = lam[n0 + k], lam[MODES + n0 + k]
                    out += [re * lr - im * li, re * li + im * lr]
                dst[at, :] = total
                return tuple(out)

            lax.fori_loop(0, SUB, body, tuple(start), unroll=4)

        follow(y, yt, False, start_f)
        follow(gp, gt, True, start_b)

    none, one = (jnp.ones_like(zero16), zero16), lam16
    yt[0:1, :] -= read_out(inv16) * p1
    gt[0:1, :] += read_out(none) * g0 + read_out(one) * g1
    gt[1:2, :] += read_out(none) * g1

    io.need(8, 10)
    og[0:ROWS, :] = og_far[...].T
    og[ROWS + 2 : EXT, :] = jnp.zeros((EXT - ROWS - 2, 128), F32)
    for k in range(3):
        ext[6:8, 128 * k : 128 * k + 128] = rim[k]
    og[ROWS : ROWS + 2, :] = nxt[3]
    for k, at_k in ((0, 2), (1, 0), (2, 1)):
        lanes = slice(128 * k, 128 * k + 128)
        br[0:ROWS, lanes] = convolve(taps, ext, k)
        br[ROWS : ROWS + 2, lanes] = nxt[at_k]
    br[ROWS + 2 : EXT, :] = jnp.zeros((EXT - ROWS - 2, 384), F32)
    prod[...] = br[:, 128:256] * br[:, 256:384]
    gl[...] = og[...] * br[:, 0:128]
    gain = skip[...]
    long_out = yt[0:EXT, :] + gain * prod[...]
    gb[:, 0:128] = og[...] * long_out
    grad_prod = gt[0:EXT, :] + gain * gl[...]
    gb[:, 128:256] = grad_prod * br[:, 256:384]
    gb[:, 256:384] = grad_prod * br[:, 128:256]
    for k in range(3):
        lanes = slice(128 * k, 128 * k + 128)
        total = None
        for j in range(3):
            term = taps[k, j : j + 1, :] * gb[j : j + ROWS, lanes]
            total = term if total is None else total + term
            row = 32 + 3 * k + j
            small[row : row + 1, :] = jnp.sum(
                gb[0:ROWS, lanes] * ext[8 - j : 8 - j + ROWS, lanes], axis=0, keepdims=True
            )
        low[0:ROWS, lanes] = total.astype(BF16)
    small[41:42, :] = jnp.sum(gl[0:ROWS, :] * prod[0:ROWS, :], axis=0, keepdims=True)
    small[42:48, :] = jnp.zeros((6, 128), F32)
    wide = jnp.concatenate([small[16 * i : 16 * i + 16, :] for i in range(3)], axis=1)
    split_rows(wide, low, ROWS)
    io.done(1)
    mixed[...] = (br[0:ROWS, 0:128] * long_out[0:ROWS, :]).T


def split_rows(wide, dst, row):
    high = wide.astype(BF16)
    dst[row : row + 16, :] = high
    dst[row + 16 : row + 32, :] = (wide - high.astype(F32)).astype(BF16)


def join_rows(src, row):
    return src[row : row + 16, :].astype(F32) + src[row + 16 : row + 32, :].astype(F32)


def input_kernel(at, low, low_core, weight, partner, out, left, lturn, right, parts, sems):
    core = at[0]
    copies = copy_all([(low.at[0:ROWS], left.at[0]), (low_core.at[0:ROWS], left.at[1])], sems)
    far = []
    for n in range(8):
        for s, src in enumerate((weight, partner)):
            c = pltpu.make_async_copy(src.at[:, n, core], right.at[n, s], sems.at[2 + 2 * n + s])
            c.start()
            far.append(c)
    wait_all(copies)
    lturn[...] = jnp.concatenate([left[0].T, left[1].T], axis=0)
    sent = []
    for n in range(0, 8, 2):
        wait_all(far[2 * n : 2 * n + 4])
        cols = [
            jnp.concatenate([right[i, s, k] for s in range(2) for k in range(3)], axis=1)
            for i in (n, n + 1)
        ]
        cols = jnp.concatenate(cols, axis=0)
        total = jnp.dot(cols, lturn[...], preferred_element_type=F32).astype(BF16)
        for i in range(2):
            parts[n + i] = total[256 * i : 256 * i + 256]
            c = pltpu.make_async_copy(parts.at[n + i], out.at[n + i], sems.at[18 + n + i])
            c.start()
            sent.append(c)
    wait_all(sent)


FAR_ORDER = (4, 3, -3, 1, -1, 2, -2, 0)
HALF = 128


def weight_kernel(at, mine, other, given, passed, low, low_y, _, *rest):
    outs, (held, cols, made, far_made, near_made, sems) = rest[:7], rest[7:]
    z = at[6]
    one, one_back, four, four_back, near, middle, own_small = outs
    far = []
    for n, d in enumerate(FAR_ORDER):
        p = lax.rem(z + (d + 8), 8)
        for s, pair in enumerate(((other, mine), (passed, given))):
            dst = held.at[n, ROWS * s : ROWS * s + ROWS]
            for flag, src in enumerate(pair):
                c = pltpu.make_async_copy(src.at[p], dst, sems.at[2 + 2 * n + s])

                @pl.when(at[3] == flag)
                def _(c=c):
                    c.start()

            far.append(c)
        if n == 0:
            copies = copy_all([(low, cols.at[0]), (low_y, cols.at[1])], sems)
    wait_all(copies)
    right = jnp.concatenate([cols[0, 0:ROWS, :], cols[1, 0:ROWS, :]], axis=0)
    wide = join_rows(cols.at[0], ROWS) + join_rows(cols.at[1], ROWS)
    for i in range(2):
        split_rows(wide, made.at[i], 512)
        split_rows(wide, far_made.at[i], HALF)
    sent = []

    def send(src, dst):
        c = pltpu.make_async_copy(src, dst, sems.at[18 + len(sent)])
        c.start()
        sent.append(c)

    send(made.at[0, 512:544], own_small)
    for n, d in enumerate(FAR_ORDER):
        if n % 2 == 0:
            wait_all(far[2 * n : 2 * n + 4])
            both = jnp.concatenate([held[n], held[n + 1]], axis=1)
            both = lax.dot_general(both, right, (((0,), (0,)), ((), ())), preferred_element_type=F32)
        total = both[256 * (n % 2) : 256 * (n % 2) + 256]
        if n == 0:
            total = total.astype(BF16)
            far_made[0, 0:HALF, :] = total[HALF:]
            far_made[1, 0:HALF, :] = total[0:HALF]
            send(far_made.at[0], four)
            send(far_made.at[1], four_back)
        elif n < 5:
            row = 0 if n < 3 else 256
            made[(n - 1) % 2, row : row + 256, :] = total.astype(BF16)
            if n >= 3:
                send(made.at[n - 3], (one, one_back)[n - 3])
        else:
            near_made[n - 5] = total
            send(near_made.at[n - 5], middle if n == 7 else near.at[n - 5])
    wait_all(sent)


def relay_kernel(near, one, four, one_back, four_back, back, ahead, io):
    io.need(0, 3, 4)
    total = near[1] + one_back[0:256, :].astype(F32)
    back[0:HALF, :] = (total[0:HALF] + four_back[0:HALF, :].astype(F32)).astype(BF16)
    back[HALF:256, :] = total[HALF:].astype(BF16)
    back[256:288, :] = one_back[512:544, :]
    back[288:320, :] = four_back[HALF : HALF + 32, :]
    io.done(0)
    io.need(1, 2)
    total = near[0] + one[0:256, :].astype(F32)
    ahead[0:HALF, :] = total[0:HALF].astype(BF16)
    ahead[HALF:256, :] = (total[HALF:] + four[0:HALF, :].astype(F32)).astype(BF16)
    ahead[256:288, :] = one[512:544, :]


def fold_input_kernel(parts, out):
    total = parts[0].astype(F32)
    for j in range(1, 8):
        total = total + parts[j].astype(F32)
    out[...] = total.T


def early_kernel(middle, one, one_back, out):
    out[...] = middle[...] + one[256:512, :].astype(F32) + one_back[256:512, :].astype(F32)


def fold_kernel(
    at, early, back, ahead, own_small, one, one_back, four, four_back, out, res, taps, skip, table, io
):
    z = at[6]
    io.need(0, 1, 2)
    total = early[...] + back[0:256, :].astype(F32) + ahead[0:256, :].astype(F32)
    for k in range(3):
        out[k] = total[:, 128 * k : 128 * k + 128]
    io.done(0)
    io.need(3, 4, 5, 6, 7)
    came = ((own_small, 0, 0), (one, 0, -1), (four, 0, -2), (ahead, 256, -3))
    came += ((one_back, 0, 1), (four_back, 0, 2), (back, 256, 3), (back, 288, 4))
    for src, row, d in came:
        table[lax.rem(z + (d + 8), 8)] = join_rows(src, row)
    wide = table[0]
    for j in range(1, 8):
        wide = wide + table[j]
    res[0] = wide[:, 0:128]
    res[1] = wide[:, 128:256]
    for k in range(3):
        taps[k] = wide[3 * k : 3 * k + 3, 256:384]
    skip[...] = wide[9:10, 256:384]


VMEM_BYTES = 64 * 1024 * 1024 - 128 * 1024
FAR = pl.BlockSpec(memory_space=pltpu.HBM)
SCALARS = pl.BlockSpec(memory_space=pltpu.SMEM)


def raw_call(kernel, us, outs, scratch, sems, args, in_specs, out_specs):
    return pl.pallas_call(
        kernel,
        in_specs=in_specs,
        out_specs=out_specs,
        out_shape=[jax.ShapeDtypeStruct(s, t) for s, t in outs],
        scratch_shapes=[pltpu.VMEM(s, t) for s, t in scratch] + [pltpu.SemaphoreType.DMA((sems,))],
        compiler_params=pltpu.CompilerParams(vmem_limit_bytes=VMEM_BYTES),
        cost_estimate=pl.CostEstimate(flops=int(us * 1.1e9), bytes_accessed=0, transcendentals=0),
    )(*args)


def far_call(kernel, us, at, outs, scratch, sems, *args):
    scalars = () if at is None else (at,)
    specs = [SCALARS] * len(scalars) + [FAR] * len(args)
    return raw_call(kernel, us, outs, scratch, sems, scalars + args, specs, [FAR] * len(outs))


class Staged:
    def __init__(self, ins, outs):
        self.ins, self.outs, self.here, self.gone = ins, outs, set(), set()

    def need(self, *which):
        for i in which:
            if i not in self.here:
                self.here.add(i)
                self.ins[i].wait()

    def done(self, *which):
        for i in which:
            if i not in self.gone:
                self.gone.add(i)
                self.outs[i].start()


def call(kernel, us, at, outs, scratch, *args, far=(), sems=0, late=(), staged=False, windows=()):
    scalars = () if at is None else (at,)
    n_s, n_f, n_i, n_l, n_o = len(scalars), len(far), len(args), len(late), len(outs)

    def body(*refs):
        refs = list(refs)

        def take(count):
            head = refs[:count]
            del refs[:count]
            return head

        top, far_refs, ins, _, results = take(n_s), take(n_f), take(n_i), take(n_l), take(n_o)
        held, made, own, sem = take(n_i), take(n_o), refs[:-1], refs[-1]

        def copies(pairs, base):
            return [pltpu.make_async_copy(a, b, sem.at[base + i]) for i, (a, b) in enumerate(pairs)]

        for i, row in windows:
            ins[i] = ins[i].at[row : row + 32]
        coming = copies(zip(ins, held), sems)
        for c in coming:
            c.start()
        io = Staged(coming, copies(zip(made, results), sems + n_i))
        if not staged:
            io.need(*range(n_i))
        extra = ((sem,) if far else ()) + ((io,) if staged else ())
        kernel(*top, *far_refs, *held, *made, *own, *extra)
        io.need(*range(n_i))
        io.done(*range(n_o))
        wait_all(io.outs)

    shapes = [(a.shape, a.dtype) for a in args]
    for i, _ in windows:
        shapes[i] = ((32, args[i].shape[1]), args[i].dtype)
    buffers = shapes + list(outs) + list(scratch)
    specs = [SCALARS] * n_s + [FAR] * (n_f + n_i + n_l)
    total = sems + n_i + n_o
    return raw_call(
        body, us, outs, buffers, total, scalars + tuple(far) + args + tuple(late), specs, [FAR] * n_o
    )


def after(x, *deps):
    return pl.pallas_call(
        lambda *_: None,
        in_specs=[pl.BlockSpec(memory_space=pl.ANY)] * (1 + len(deps)),
        out_specs=pl.BlockSpec(memory_space=pl.ANY),
        out_shape=jax.ShapeDtypeStruct(x.shape, x.dtype),
        input_output_aliases={0: 0},
    )(x, *deps)


CHIPS = [[x * 4 + y * 2 + c for x in range(4) for y in range(2)] for c in range(2)]
COLUMNS = [[z * 2 + y for z in range(8)] for y in range(2)]


def exchange(x, axis, groups=None):
    return lax.all_to_all(
        x, axis, split_axis=0, concat_axis=0, tiled=True, axis_index_groups=groups
    )


def joint_pairs(kind):
    pairs = []
    for s in range(16):
        for c in range(16):
            wanted = s % 2 == c % 2
            if kind == "give" and not wanted:
                pairs.append((s * 16 + c, (s ^ 1) * 16 + c))
            if kind == "pass" and wanted:
                pairs.append((s * 16 + c, s * 16 + (c ^ 1)))
    return pairs


def on_device(
    hidden_in, in_weight, conv_taps, decay_rate, mode_angle, residue, skip_gain, out_grad
):
    chan, seq = lax.axis_index("chan"), lax.axis_index("seq")
    core, yl = chan % 2, seq % 2
    same = (yl == core).astype(jnp.int32)
    at = jnp.stack([core, chan, seq, same, chan // 4, chan // 2 % 2, seq // 2]).astype(jnp.int32)

    mine = exchange(jnp.broadcast_to(hidden_in[None], (8, ROWS, 256)), "chan", CHIPS)
    partner = to_chan(in_weight, 0, 0, 1)

    away = jnp.abs(jnp.arange(16, dtype=jnp.int32) - seq).astype(F32) - 1.0
    counts = jnp.concatenate([jnp.array(COUNTS, F32), jnp.maximum(away, 0.0) * float(ROWS)])
    pw = pole_power(decay_rate[None], mode_angle[None], counts[:, None, None])
    pw = jnp.concatenate(pw, axis=1)
    res = residue.reshape(2 * MODES, 128)

    mine = after(mine, pw, at)
    other = to_chan(mine, 0, 0, 1)
    weight = in_weight.reshape(3, 8, 2, 256, 128)
    block, wblock = ((8, ROWS, 256), BF16), ((3, 8, 256, 128), BF16)
    half = far_call(
        half_kernel, 4.0, at, [((ROWS, 384), F32)], [block, wblock, ((ROWS, 384), F32)], 48, mine, weight
    )[0]
    given = lax.ppermute(mine, ("seq", "chan"), joint_pairs("give"))
    ext, prod, gl, st, send = call(
        states_kernel,
        8.0,
        at,
        [((528, 384), F32), ((SPAN, 128), F32), ((SPAN, 128), F32), ((64, 8, 128), F32), ((16, 48, 128), F32)],
        [block, wblock, ((64, 128), F32)] + [((32, 8, 128), F32)] * 3,
        half, conv_taps, out_grad, pw,
        far=(other, weight),
        sems=48,
        staged=True,
    )
    arrived = exchange(send, "seq")
    y, gp, sums = call(
        scan_kernel,
        7.0,
        None,
        [((SUB, 8, 128), F32)] * 2 + [((96, 8, 128), F32)],
        [((32, 8, 128), F32)] * 2,
        prod, gl, st, pw, res,
    )
    given = after(given, arrived, y)
    passed = lax.ppermute(given, ("seq", "chan"), joint_pairs("pass"))
    mixed_out, low = call(
        grads_kernel,
        8.0,
        at,
        [((128, ROWS), F32), ((ROWS + 32, 384), BF16)],
        [((SPAN, 128), F32), ((SPAN, 128), F32), ((EXT, 384), F32), ((EXT, 384), F32)]
        + [((EXT, 128), F32), ((EXT, 128), F32), ((48, 128), F32), ((EXT, 128), F32)]
        + [((32, 8, 128), F32)] * 4,
        arrived, pw, res, skip_gain[None, :], y, gp, sums, st, ext, conv_taps, out_grad,
        staged=True,
    )

    low_y = to_seq(low, 0, 1)
    low_core = to_chan(low, 0, 0, 1)
    terms = far_call(
        input_kernel,
        6.0,
        at,
        [((8, 256, ROWS), BF16)],
        [((2, ROWS, 384), BF16), ((768, ROWS), BF16), ((8, 2, 3, 256, 128), BF16), ((8, 256, ROWS), BF16)],
        26,
        low, low_core, weight, partner.reshape(weight.shape),
    )[0]
    pair_rows, half_rows = ((544, 384), BF16), ((HALF + 32, 384), BF16)
    one, one_back, four, four_back, near, middle, own_small = far_call(
        weight_kernel,
        40.0,
        at,
        [pair_rows] * 2 + [half_rows] * 2
        + [((2, 256, 384), F32), ((256, 384), F32), ((32, 384), BF16)],
        [((8, 2 * ROWS, 256), BF16), ((2, ROWS + 32, 384), BF16), ((2, 544, 384), BF16)]
        + [((2, HALF + 32, 384), BF16), ((3, 256, 384), F32)],
        28,
        mine, other, given, passed, low, low_y, terms,
    )
    terms = exchange(terms, "chan", CHIPS)
    four, four_back = to_seq(four, 2), to_seq(four_back, -2)
    one, one_back = to_seq(one, 1), to_seq(one_back, -1)
    back, ahead = call(
        relay_kernel,
        2.0,
        None,
        [((320, 384), BF16), ((288, 384), BF16)],
        [],
        near, one, four, one_back, four_back,
        staged=True,
    )
    back, ahead = to_seq(back, -2), to_seq(ahead, 2)
    input_grad = call(fold_input_kernel, 2.5, None, [((ROWS, 256), F32)], [], terms)[0]
    early = call(early_kernel, 2.0, None, [((256, 384), F32)], [], middle, one, one_back)[0]
    weight_grad, residue_grad, taps_grad, skip_grad = call(
        fold_kernel,
        2.5,
        at,
        [((3, 256, 128), F32), ((2, MODES, 128), F32), ((3, 3, 128), F32), ((1, 128), F32)],
        [((8, 16, 384), F32)],
        early, back, ahead, own_small, one, one_back, four, four_back,
        windows=((4, 512), (5, 512), (6, HALF), (7, HALF)),
        late=(input_grad,),
        staged=True,
    )
    return (mixed_out, input_grad, weight_grad, taps_grad, residue_grad, skip_grad.reshape(128))


def solution(mesh):
    in_specs = (
        P("seq", "chan"),
        P(None, None, "chan"),
        P(None, None, "chan"),
        P(None, "chan"),
        P(None, "chan"),
        P(None, None, "chan"),
        P("chan"),
        P("chan", "seq"),
    )
    out_specs = (
        P("chan", "seq"),
        P("seq", "chan"),
        P(None, "seq", "chan"),
        P(None, None, "chan"),
        P(None, None, "chan"),
        P("chan"),
    )
    return jax.shard_map(
        on_device, mesh=mesh, in_specs=in_specs, out_specs=out_specs, check_vma=False
    )
```

```python
import jax
import jax.numpy as jnp
from jax import lax
from jax.experimental import pallas as pl
from jax.experimental.pallas import tpu as pltpu
from jax.sharding import PartitionSpec as P

F32 = jnp.float32
BF16 = jnp.bfloat16
MODES = 16
SUB = 64
ROWS = 8 * SUB
EXT = ROWS + 8
SPAN = ROWS + SUB


def chan_pairs(dx, dy, dc):
    pairs = []
    for c in range(16):
        x, y, core = c // 4, c // 2 % 2, c % 2
        pairs.append((c, (x + dx) % 4 * 4 + (y + dy) % 2 * 2 + (core + dc) % 2))
    return pairs


def seq_pairs(dz, dy):
    return [(s, (s // 2 + dz) % 8 * 2 + (s % 2 + dy) % 2) for s in range(16)]


def to_chan(x, dx, dy, dc=0):
    return lax.ppermute(x, "chan", chan_pairs(dx, dy, dc))


def to_seq(x, dz, dy=0):
    return lax.ppermute(x, "seq", seq_pairs(dz, dy))


def pole_power(rate, angle, count):
    high = jnp.round(angle * 1024.0) * (1.0 / 1024.0)
    low = angle - high
    one, two = high * count, low * count
    mag = jnp.exp(-rate * count)
    cos1, sin1, cos2, sin2 = jnp.cos(one), jnp.sin(one), jnp.cos(two), jnp.sin(two)
    return mag * (cos1 * cos2 - sin1 * sin2), mag * (sin1 * cos2 + cos1 * sin2)


COUNTS = (1.0, -1.0, float(ROWS), float(ROWS - 1), float(ROWS - 2), float(SUB), float(2 * SUB), float(4 * SUB))


def halves(ref, row=None):
    if row is None:
        return ref[0:MODES, :], ref[MODES : 2 * MODES, :]
    return ref[row, 0:MODES, :], ref[row, MODES : 2 * MODES, :]


def fill(pw, rows, dst):
    for n in range(2 * MODES):
        line = rows[n : n + 1, :] if pw is None else pw[rows, n : n + 1, :]
        dst[n] = jnp.broadcast_to(line, (8, 128))


def sub_powers(pw, dst, back):
    place = lax.broadcasted_iota(jnp.int32, (8, 128), 0)
    place = 7 - place if back else place
    for n in range(MODES):
        re, im = jnp.ones((8, 128), F32), jnp.zeros((8, 128), F32)
        for level in range(3):
            here = (place >> level) & 1 == 1
            step = pw[5 + level, n : n + 1, :], pw[5 + level, MODES + n : MODES + n + 1, :]
            step = tuple(jnp.where(here, s, t) for s, t in zip(step, (1.0, 0.0)))
            re, im = times((re, im), step)
        dst[n] = re
        dst[MODES + n] = im


def times(a, b):
    return a[0] * b[0] - a[1] * b[1], a[0] * b[1] + a[1] * b[0]


def copy_all(pairs, sems):
    copies = [pltpu.make_async_copy(a, b, sems.at[i]) for i, (a, b) in enumerate(pairs)]
    for c in copies:
        c.start()
    return copies


def wait_all(copies, start=False):
    for c in copies:
        if start:
            c.start()
        c.wait()


def stream(sources, weight_far, par, held, weight, sems):
    copies = []
    for b in range(8):
        pairs = [(weight_far.at[:, b, par], weight.at[:, b])]
        pairs += [(src.at[b], dst.at[b]) for src, dst in zip(sources, held)]
        group = [pltpu.make_async_copy(f, t, sems.at[6 * b + i]) for i, (f, t) in enumerate(pairs)]
        for c in group:
            c.start()
        copies.append(group)
    return copies


def columns(weight, b):
    return jnp.concatenate([weight[k, b] for k in range(3)], axis=1)


def convolve(taps, ext, k):
    lanes = slice(128 * k, 128 * k + 128)
    total = taps[k, 0:1, :] * ext[8 : 8 + ROWS, lanes]
    total = total + taps[k, 1:2, :] * ext[7 : 7 + ROWS, lanes]
    return total + taps[k, 2:3, :] * ext[6 : 6 + ROWS, lanes]


def half_kernel(at, mine_far, weight_far, _, out, mine, weight, made, sems):
    copies = stream([mine_far], weight_far, at[0], [mine], weight, sems)
    for b in range(0, 8, 2):
        for i in range(b, b + 2):
            wait_all(copies[i])
        left = jnp.concatenate([mine[i] for i in range(b, b + 2)], axis=1)
        right = jnp.concatenate([columns(weight, i) for i in range(b, b + 2)], axis=0)
        total = jnp.dot(left, right, preferred_element_type=F32)
        made[...] = total if b == 0 else made[...] + total
    wait_all([pltpu.make_async_copy(made, out, sems.at[0])], start=True)


def states_kernel(
    at, other_far, weight_far, half, taps, og, pw,
    ext, prod, gl, st, send, other, weight, ends, lam, pwf, pwb, sems, io,
):
    seq = at[2]
    copies = stream([other_far], weight_far, 1 - at[0], [other], weight, sems)
    io.need(3)
    fill(pw, 0, lam)
    sub_powers(pw, pwf, True)
    sub_powers(pw, pwb, False)
    for b in range(0, 8, 2):
        for i in range(b, b + 2):
            wait_all(copies[i])
        left = jnp.concatenate([other[i] for i in range(b, b + 2)], axis=1)
        right = jnp.concatenate([columns(weight, i) for i in range(b, b + 2)], axis=0)
        total = jnp.dot(left, right, preferred_element_type=F32)
        if b == 0:
            io.need(0)
        ext[8:520, :] = (half[...] if b == 0 else ext[8:520, :]) + total
    ext[0:8, :] = jnp.zeros((8, 384), F32)
    ext[520:528, :] = jnp.zeros((8, 384), F32)
    io.done(0)
    io.need(1, 2)
    q, k, v = (convolve(taps, ext, i) for i in range(3))
    fresh = lax.broadcasted_iota(jnp.int32, (ROWS, 128), 0) >= 2
    prod[0:ROWS, :] = jnp.where(fresh, k * v, 0.0)
    cot = og[...].T
    gl[0:ROWS, :] = jnp.where(fresh, cot * q, 0.0)
    io.done(1, 2)
    edge = [k[0:2], v[0:2], q[0:2], cot[0:2]]
    edge += [ext[518:520, 128 * i : 128 * i + 128] for i in range(3)]
    edge = jnp.concatenate(edge + [jnp.zeros((2, 128), F32)], axis=0)
    half = MODES // 2
    for src, powers, back, base in ((prod, pwf, False, 0), (gl, pwb, True, 32)):
        for n0 in range(0, MODES, half):

            def body(step, carry, n0=n0, back=back, src=src):
                i = SUB - 1 - step if back else step
                v = src[pl.ds(i, 8, stride=SUB), :]
                out = []
                for k in range(half):
                    re, im = carry[2 * k], carry[2 * k + 1]
                    lr, li = lam[n0 + k], lam[MODES + n0 + k]
                    out += [re * lr - im * li + v, re * li + im * lr]
                return tuple(out)

            zero = tuple(jnp.zeros((8, 128), F32) for _ in range(2 * half))
            carry = lax.fori_loop(0, SUB, body, zero, unroll=4)
            for k in range(half):
                n = n0 + k
                re, im = carry[2 * k], carry[2 * k + 1]
                st[base + n] = re
                st[base + MODES + n] = im
                er, ei = times((re, im), (powers[n], powers[MODES + n]))
                ends[base + n : base + n + 1, :] = jnp.sum(er, axis=0, keepdims=True)
                ends[base + MODES + n : base + MODES + n + 1, :] = jnp.sum(ei, axis=0, keepdims=True)
    io.done(3)
    for j in range(16):
        send[j, 0:32, :] = jnp.where(j >= seq, ends[0:32, :], ends[32:64, :])
        send[j, 32:48, :] = edge


def scan_kernel(prod, gl, st, pw, res, y, gp, sums, lam, rho):
    fill(pw, 0, lam)
    fill(None, res, rho)
    half = MODES // 2
    place = lax.broadcasted_iota(jnp.int32, (8, 128), 0)
    for base, back in ((0, False), (32, True)):
        for n in range(MODES):

            def shift(v, by, back=back):
                moved = pltpu.roll(v, 8 - by if back else by, 0)
                return jnp.where(place < 8 - by if back else place >= by, moved, 0.0)

            re, im = shift(st[base + n], 1), shift(st[base + MODES + n], 1)
            for level, by in enumerate((1, 2, 4)):
                ar, ai = times(
                    (shift(re, by), shift(im, by)),
                    (pw[5 + level, n : n + 1, :], pw[5 + level, MODES + n : MODES + n + 1, :]),
                )
                re, im = re + ar, im + ai
            sums[32 + base + n] = re
            sums[32 + base + MODES + n] = im
    for n0 in range(0, MODES, half):

        def forward(step, carry, n0=n0):
            p = prod[pl.ds(step, 8, stride=SUB), :]
            g = gl[pl.ds(step, 8, stride=SUB), :]
            out = []
            total = None
            for k in range(half):
                re, im, sr, si = carry[4 * k : 4 * k + 4]
                lr, li = lam[n0 + k], lam[MODES + n0 + k]
                re, im = re * lr - im * li + p, re * li + im * lr
                term = re * rho[n0 + k] - im * rho[MODES + n0 + k]
                total = term if total is None else total + term
                out += [re, im, sr + g * re, si + g * im]
            y[step] = total if n0 == 0 else y[step] + total
            return tuple(out)

        zero = tuple(jnp.zeros((8, 128), F32) for _ in range(4 * half))
        carry = lax.fori_loop(0, SUB, forward, zero, unroll=4)
        for k in range(half):
            sums[n0 + k] = carry[4 * k + 2]
            sums[MODES + n0 + k] = carry[4 * k + 3]

        def backward(step, carry, n0=n0):
            i = SUB - 1 - step
            g = gl[pl.ds(i, 8, stride=SUB), :]
            out = []
            total = None
            for k in range(half):
                re, im = carry[2 * k : 2 * k + 2]
                lr, li = lam[n0 + k], lam[MODES + n0 + k]
                re, im = re * lr - im * li + g, re * li + im * lr
                term = re * rho[n0 + k] - im * rho[MODES + n0 + k]
                total = term if total is None else total + term
                out += [re, im]
            gp[i] = total if n0 == 0 else gp[i] + total
            return tuple(out)

        zero = tuple(jnp.zeros((8, 128), F32) for _ in range(2 * half))
        lax.fori_loop(0, SUB, backward, zero, unroll=4)


def grads_kernel(
    at, arrived, pw, res, skip, y, gp, sums, st, ext, taps, og_far,
    mixed, low, yt, gt, gb, br, prod, gl, small, og, lam, rho, pwf, pwb, io,
):
    seq = at[2]

    io.need(1, 2, 9)
    fill(pw, 0, lam)
    fill(None, res, rho)
    sub_powers(pw, pwf, True)
    sub_powers(pw, pwb, False)
    lam16, inv16, lam512, lam511, lam510 = (halves(pw, i) for i in range(5))
    rho16 = halves(res)
    io.need(0, 3)
    zero16 = jnp.zeros((MODES, 128), F32)
    s_in, u_in = (zero16, zero16), (zero16, zero16)
    zero2 = jnp.zeros((2, 128), F32)
    own = nxt = [zero2] * 6
    rim = [zero2] * 3
    first = lax.broadcasted_iota(jnp.int32, (2, 128), 0) == 0

    def choose(flag, new, old):
        return [jnp.where(flag, a, b) for a, b in zip(new, old)]

    before = [zero2] * 3
    for j in range(16):
        tilde = arrived[j, 32:40, :]
        kvq = []
        for k, rows in ((1, tilde[0:2]), (2, tilde[2:4]), (0, tilde[4:6])):
            t1, t2 = taps[k, 1:2, :], taps[k, 2:3, :]
            p2, p1 = before[k][0:1], before[k][1:2]
            kvq.append(rows + jnp.where(first, t1 * p1 + t2 * p2, t2 * p1))
        out_grad = tilde[6:8]
        product = kvq[0] * kvq[1]
        cotangent = out_grad * kvq[2]
        mine = kvq + [out_grad, product, cotangent]
        tail = arrived[j, 40:48, :]
        before = [tail[0:2], tail[2:4], tail[4:6]]
        own = choose(j == seq, mine, own)
        nxt = choose(j == seq + 1, mine, nxt)
        rim = choose(j == seq - 1, before, rim)
        got = halves(arrived, j)
        p0, p1 = product[0:1], product[1:2]
        g0, g1 = cotangent[0:1], cotangent[1:2]
        ahead = j < seq
        fixed = [
            got[i] + jnp.where(ahead, lam511[i] * p0 + lam510[i] * p1, lam16[i] * g1 + (g0 if i == 0 else 0.0))
            for i in range(2)
        ]
        re, im = times(fixed, halves(pw, 8 + j))
        behind = j > seq
        s_in = (s_in[0] + jnp.where(ahead, re, 0.0), s_in[1] + jnp.where(ahead, im, 0.0))
        u_in = (u_in[0] + jnp.where(behind, re, 0.0), u_in[1] + jnp.where(behind, im, 0.0))

    def read_out(state):
        return jnp.sum(rho16[0] * state[0] - rho16[1] * state[1], axis=0, keepdims=True)

    p0, p1, g0, g1 = own[4][0:1], own[4][1:2], own[5][0:1], own[5][1:2]
    x0 = times(lam16, s_in)
    x0 = (x0[0] + p0, x0[1])
    x1 = times(lam16, x0)
    x1 = (x1[0] + p1, x1[1])
    small[0:16, :] = g0 * x0[0] + g1 * x1[0]
    small[16:32, :] = -(g0 * x0[1] + g1 * x1[1])
    inv2 = times(inv16, inv16)
    s_in = tuple(s_in[i] + inv16[i] * p0 + inv2[i] * p1 for i in range(2))
    carried = times(lam512, s_in)
    last = halves(arrived, seq)
    last = (last[0] + carried[0], last[1] + carried[1])
    for extra in range(2):
        moved = times(lam16, last)
        last = (moved[0] + nxt[4][extra : extra + 1], moved[1])
        yt[ROWS + extra : ROWS + extra + 1, :] = read_out(last)
    gt[ROWS : ROWS + 1, :] = read_out(u_in)
    later = times(inv16, (u_in[0] - nxt[5][0:1], u_in[1]))
    gt[ROWS + 1 : ROWS + 2, :] = read_out(later)
    yt[ROWS + 2 : EXT, :] = jnp.zeros((EXT - ROWS - 2, 128), F32)
    gt[ROWS + 2 : EXT, :] = jnp.zeros((EXT - ROWS - 2, 128), F32)
    io.need(4, 5, 6, 7)

    half = MODES // 2
    for n0 in range(0, MODES, half):
        start_f, start_b = [], []
        for k in range(half):
            n = n0 + k
            l8 = (lam[n], lam[MODES + n])
            r8 = (rho[n], rho[MODES + n])

            def full(state, powers, base, n=n):
                wide = tuple(jnp.broadcast_to(s[n : n + 1, :], (8, 128)) for s in state)
                add = times(wide, (powers[n], powers[MODES + n]))
                return times((sums[base + n] + add[0], sums[base + MODES + n] + add[1]), l8)

            q = full(s_in, pwb, 32)
            rr, ri = times(q, (st[32 + n], st[48 + n]))
            small[n : n + 1, :] += jnp.sum(sums[n] + rr, axis=0, keepdims=True)
            small[MODES + n : MODES + n + 1, :] -= jnp.sum(sums[MODES + n] + ri, axis=0, keepdims=True)
            start_f += list(times(q, r8))
            start_b += list(times(full(u_in, pwf, 64), r8))

        def follow(src, dst, back, start, n0=n0):
            def body(step, carry):
                i = SUB - 1 - step if back else step
                at = pl.ds(i, 8, stride=SUB)
                total = src[i] if n0 == 0 else dst[at, :]
                out = []
                for k in range(half):
                    re, im = carry[2 * k], carry[2 * k + 1]
                    total = total + re
                    lr, li = lam[n0 + k], lam[MODES + n0 + k]
                    out += [re * lr - im * li, re * li + im * lr]
                dst[at, :] = total
                return tuple(out)

            lax.fori_loop(0, SUB, body, tuple(start), unroll=4)

        follow(y, yt, False, start_f)
        follow(gp, gt, True, start_b)

    none, one = (jnp.ones_like(zero16), zero16), lam16
    yt[0:1, :] -= read_out(inv16) * p1
    gt[0:1, :] += read_out(none) * g0 + read_out(one) * g1
    gt[1:2, :] += read_out(none) * g1

    io.need(8, 10)
    og[0:ROWS, :] = og_far[...].T
    og[ROWS + 2 : EXT, :] = jnp.zeros((EXT - ROWS - 2, 128), F32)
    for k in range(3):
        ext[6:8, 128 * k : 128 * k + 128] = rim[k]
    og[ROWS : ROWS + 2, :] = nxt[3]
    for k, at_k in ((0, 2), (1, 0), (2, 1)):
        lanes = slice(128 * k, 128 * k + 128)
        br[0:ROWS, lanes] = convolve(taps, ext, k)
        br[ROWS : ROWS + 2, lanes] = nxt[at_k]
    br[ROWS + 2 : EXT, :] = jnp.zeros((EXT - ROWS - 2, 384), F32)
    prod[...] = br[:, 128:256] * br[:, 256:384]
    gl[...] = og[...] * br[:, 0:128]
    gain = skip[...]
    long_out = yt[0:EXT, :] + gain * prod[...]
    gb[:, 0:128] = og[...] * long_out
    grad_prod = gt[0:EXT, :] + gain * gl[...]
    gb[:, 128:256] = grad_prod * br[:, 256:384]
    gb[:, 256:384] = grad_prod * br[:, 128:256]
    for k in range(3):
        lanes = slice(128 * k, 128 * k + 128)
        total = None
        for j in range(3):
            term = taps[k, j : j + 1, :] * gb[j : j + ROWS, lanes]
            total = term if total is None else total + term
            row = 32 + 3 * k + j
            small[row : row + 1, :] = jnp.sum(
                gb[0:ROWS, lanes] * ext[8 - j : 8 - j + ROWS, lanes], axis=0, keepdims=True
            )
        low[0:ROWS, lanes] = total.astype(BF16)
    small[41:42, :] = jnp.sum(gl[0:ROWS, :] * prod[0:ROWS, :], axis=0, keepdims=True)
    small[42:48, :] = jnp.zeros((6, 128), F32)
    wide = jnp.concatenate([small[16 * i : 16 * i + 16, :] for i in range(3)], axis=1)
    split_rows(wide, low, ROWS)
    io.done(1)
    mixed[...] = (br[0:ROWS, 0:128] * long_out[0:ROWS, :]).T


def split_rows(wide, dst, row):
    high = wide.astype(BF16)
    dst[row : row + 16, :] = high
    dst[row + 16 : row + 32, :] = (wide - high.astype(F32)).astype(BF16)


def join_rows(src, row):
    return src[row : row + 16, :].astype(F32) + src[row + 16 : row + 32, :].astype(F32)


def input_kernel(at, low, low_core, weight, partner, out, left, lturn, right, parts, sems):
    core = at[0]
    copies = copy_all([(low.at[0:ROWS], left.at[0]), (low_core.at[0:ROWS], left.at[1])], sems)
    far = []
    for n in range(8):
        for s, src in enumerate((weight, partner)):
            c = pltpu.make_async_copy(src.at[:, n, core], right.at[n, s], sems.at[2 + 2 * n + s])
            c.start()
            far.append(c)
    wait_all(copies)
    lturn[...] = jnp.concatenate([left[0].T, left[1].T], axis=0)
    sent = []
    for n in range(0, 8, 2):
        wait_all(far[2 * n : 2 * n + 4])
        cols = [
            jnp.concatenate([right[i, s, k] for s in range(2) for k in range(3)], axis=1)
            for i in (n, n + 1)
        ]
        cols = jnp.concatenate(cols, axis=0)
        total = jnp.dot(cols, lturn[...], preferred_element_type=F32).astype(BF16)
        for i in range(2):
            parts[n + i] = total[256 * i : 256 * i + 256]
            c = pltpu.make_async_copy(parts.at[n + i], out.at[n + i], sems.at[18 + n + i])
            c.start()
            sent.append(c)
    wait_all(sent)


FAR_ORDER = (4, 3, -3, 1, -1, 2, -2, 0)
HALF = 128


def weight_kernel(at, mine, other, given, passed, low, low_y, _, *rest):
    outs, (held, cols, made, far_made, near_made, sems) = rest[:7], rest[7:]
    z = at[6]
    one, one_back, four, four_back, near, middle, own_small = outs
    far = []
    for n, d in enumerate(FAR_ORDER):
        p = lax.rem(z + (d + 8), 8)
        for s, pair in enumerate(((other, mine), (passed, given))):
            dst = held.at[n, ROWS * s : ROWS * s + ROWS]
            for flag, src in enumerate(pair):
                c = pltpu.make_async_copy(src.at[p], dst, sems.at[2 + 2 * n + s])

                @pl.when(at[3] == flag)
                def _(c=c):
                    c.start()

            far.append(c)
        if n == 0:
            copies = copy_all([(low, cols.at[0]), (low_y, cols.at[1])], sems)
    wait_all(copies)
    right = jnp.concatenate([cols[0, 0:ROWS, :], cols[1, 0:ROWS, :]], axis=0)
    wide = join_rows(cols.at[0], ROWS) + join_rows(cols.at[1], ROWS)
    for i in range(2):
        split_rows(wide, made.at[i], 512)
        split_rows(wide, far_made.at[i], HALF)
    sent = []

    def send(src, dst):
        c = pltpu.make_async_copy(src, dst, sems.at[18 + len(sent)])
        c.start()
        sent.append(c)

    send(made.at[0, 512:544], own_small)
    for n, d in enumerate(FAR_ORDER):
        if n % 2 == 0:
            wait_all(far[2 * n : 2 * n + 4])
            both = jnp.concatenate([held[n], held[n + 1]], axis=1)
            both = lax.dot_general(both, right, (((0,), (0,)), ((), ())), preferred_element_type=F32)
        total = both[256 * (n % 2) : 256 * (n % 2) + 256]
        if n == 0:
            total = total.astype(BF16)
            far_made[0, 0:HALF, :] = total[HALF:]
            far_made[1, 0:HALF, :] = total[0:HALF]
            send(far_made.at[0], four)
            send(far_made.at[1], four_back)
        elif n < 5:
            row = 0 if n < 3 else 256
            made[(n - 1) % 2, row : row + 256, :] = total.astype(BF16)
            if n >= 3:
                send(made.at[n - 3], (one, one_back)[n - 3])
        else:
            near_made[n - 5] = total
            send(near_made.at[n - 5], middle if n == 7 else near.at[n - 5])
    wait_all(sent)


def relay_kernel(near, one, four, one_back, four_back, back, ahead, io):
    io.need(0, 3, 4)
    total = near[1] + one_back[0:256, :].astype(F32)
    back[0:HALF, :] = (total[0:HALF] + four_back[0:HALF, :].astype(F32)).astype(BF16)
    back[HALF:256, :] = total[HALF:].astype(BF16)
    back[256:288, :] = one_back[512:544, :]
    back[288:320, :] = four_back[HALF : HALF + 32, :]
    io.done(0)
    io.need(1, 2)
    total = near[0] + one[0:256, :].astype(F32)
    ahead[0:HALF, :] = total[0:HALF].astype(BF16)
    ahead[HALF:256, :] = (total[HALF:] + four[0:HALF, :].astype(F32)).astype(BF16)
    ahead[256:288, :] = one[512:544, :]


def fold_input_kernel(parts, out):
    total = parts[0].astype(F32)
    for j in range(1, 8):
        total = total + parts[j].astype(F32)
    out[...] = total.T


def early_kernel(middle, one, one_back, out):
    out[...] = middle[...] + one[256:512, :].astype(F32) + one_back[256:512, :].astype(F32)


def fold_kernel(
    at, early, back, ahead, own_small, one, one_back, four, four_back, out, res, taps, skip, table, io
):
    z = at[6]
    io.need(0, 1, 2)
    total = early[...] + back[0:256, :].astype(F32) + ahead[0:256, :].astype(F32)
    for k in range(3):
        out[k] = total[:, 128 * k : 128 * k + 128]
    io.done(0)
    io.need(3, 4, 5, 6, 7)
    came = ((own_small, 0, 0), (one, 0, -1), (four, 0, -2), (ahead, 256, -3))
    came += ((one_back, 0, 1), (four_back, 0, 2), (back, 256, 3), (back, 288, 4))
    for src, row, d in came:
        table[lax.rem(z + (d + 8), 8)] = join_rows(src, row)
    wide = table[0]
    for j in range(1, 8):
        wide = wide + table[j]
    res[0] = wide[:, 0:128]
    res[1] = wide[:, 128:256]
    for k in range(3):
        taps[k] = wide[3 * k : 3 * k + 3, 256:384]
    skip[...] = wide[9:10, 256:384]


VMEM_BYTES = 64 * 1024 * 1024 - 128 * 1024
FAR = pl.BlockSpec(memory_space=pltpu.HBM)
SCALARS = pl.BlockSpec(memory_space=pltpu.SMEM)


def raw_call(kernel, us, outs, scratch, sems, args, in_specs, out_specs):
    return pl.pallas_call(
        kernel,
        in_specs=in_specs,
        out_specs=out_specs,
        out_shape=[jax.ShapeDtypeStruct(s, t) for s, t in outs],
        scratch_shapes=[pltpu.VMEM(s, t) for s, t in scratch] + [pltpu.SemaphoreType.DMA((sems,))],
        compiler_params=pltpu.CompilerParams(vmem_limit_bytes=VMEM_BYTES),
        cost_estimate=pl.CostEstimate(flops=int(us * 1.1e9), bytes_accessed=0, transcendentals=0),
    )(*args)


def far_call(kernel, us, at, outs, scratch, sems, *args):
    scalars = () if at is None else (at,)
    specs = [SCALARS] * len(scalars) + [FAR] * len(args)
    return raw_call(kernel, us, outs, scratch, sems, scalars + args, specs, [FAR] * len(outs))


class Staged:
    def __init__(self, ins, outs):
        self.ins, self.outs, self.here, self.gone = ins, outs, set(), set()

    def need(self, *which):
        for i in which:
            if i not in self.here:
                self.here.add(i)
                self.ins[i].wait()

    def done(self, *which):
        for i in which:
            if i not in self.gone:
                self.gone.add(i)
                self.outs[i].start()


def call(kernel, us, at, outs, scratch, *args, far=(), sems=0, late=(), staged=False, windows=()):
    scalars = () if at is None else (at,)
    n_s, n_f, n_i, n_l, n_o = len(scalars), len(far), len(args), len(late), len(outs)

    def body(*refs):
        refs = list(refs)

        def take(count):
            head = refs[:count]
            del refs[:count]
            return head

        top, far_refs, ins, _, results = take(n_s), take(n_f), take(n_i), take(n_l), take(n_o)
        held, made, own, sem = take(n_i), take(n_o), refs[:-1], refs[-1]

        def copies(pairs, base):
            return [pltpu.make_async_copy(a, b, sem.at[base + i]) for i, (a, b) in enumerate(pairs)]

        for i, row in windows:
            ins[i] = ins[i].at[row : row + 32]
        coming = copies(zip(ins, held), sems)
        for c in coming:
            c.start()
        io = Staged(coming, copies(zip(made, results), sems + n_i))
        if not staged:
            io.need(*range(n_i))
        extra = ((sem,) if far else ()) + ((io,) if staged else ())
        kernel(*top, *far_refs, *held, *made, *own, *extra)
        io.need(*range(n_i))
        io.done(*range(n_o))
        wait_all(io.outs)

    shapes = [(a.shape, a.dtype) for a in args]
    for i, _ in windows:
        shapes[i] = ((32, args[i].shape[1]), args[i].dtype)
    buffers = shapes + list(outs) + list(scratch)
    specs = [SCALARS] * n_s + [FAR] * (n_f + n_i + n_l)
    total = sems + n_i + n_o
    return raw_call(
        body, us, outs, buffers, total, scalars + tuple(far) + args + tuple(late), specs, [FAR] * n_o
    )


def after(x, *deps):
    return pl.pallas_call(
        lambda *_: None,
        in_specs=[pl.BlockSpec(memory_space=pl.ANY)] * (1 + len(deps)),
        out_specs=pl.BlockSpec(memory_space=pl.ANY),
        out_shape=jax.ShapeDtypeStruct(x.shape, x.dtype),
        input_output_aliases={0: 0},
    )(x, *deps)


CHIPS = [[x * 4 + y * 2 + c for x in range(4) for y in range(2)] for c in range(2)]
COLUMNS = [[z * 2 + y for z in range(8)] for y in range(2)]


def exchange(x, axis, groups=None):
    return lax.all_to_all(
        x, axis, split_axis=0, concat_axis=0, tiled=True, axis_index_groups=groups
    )


def joint_pairs(kind):
    pairs = []
    for s in range(16):
        for c in range(16):
            wanted = s % 2 == c % 2
            if kind == "give" and not wanted:
                pairs.append((s * 16 + c, (s ^ 1) * 16 + c))
            if kind == "pass" and wanted:
                pairs.append((s * 16 + c, s * 16 + (c ^ 1)))
    return pairs


def on_device(
    hidden_in, in_weight, conv_taps, decay_rate, mode_angle, residue, skip_gain, out_grad
):
    chan, seq = lax.axis_index("chan"), lax.axis_index("seq")
    core, yl = chan % 2, seq % 2
    same = (yl == core).astype(jnp.int32)
    at = jnp.stack([core, chan, seq, same, chan // 4, chan // 2 % 2, seq // 2]).astype(jnp.int32)

    mine = exchange(jnp.broadcast_to(hidden_in[None], (8, ROWS, 256)), "chan", CHIPS)
    partner = to_chan(in_weight, 0, 0, 1)

    away = jnp.abs(jnp.arange(16, dtype=jnp.int32) - seq).astype(F32) - 1.0
    counts = jnp.concatenate([jnp.array(COUNTS, F32), jnp.maximum(away, 0.0) * float(ROWS)])
    pw = pole_power(decay_rate[None], mode_angle[None], counts[:, None, None])
    pw = jnp.concatenate(pw, axis=1)
    res = residue.reshape(2 * MODES, 128)

    other = to_chan(mine, 0, 0, 1)
    weight = in_weight.reshape(3, 8, 2, 256, 128)
    block, wblock = ((8, ROWS, 256), BF16), ((3, 8, 256, 128), BF16)
    half = far_call(
        half_kernel, 4.0, at, [((ROWS, 384), F32)], [block, wblock, ((ROWS, 384), F32)], 48, mine, weight, pw
    )[0]
    given = lax.ppermute(mine, ("seq", "chan"), joint_pairs("give"))
    ext, prod, gl, st, send = call(
        states_kernel,
        8.0,
        at,
        [((528, 384), F32), ((SPAN, 128), F32), ((SPAN, 128), F32), ((64, 8, 128), F32), ((16, 48, 128), F32)],
        [block, wblock, ((64, 128), F32)] + [((32, 8, 128), F32)] * 3,
        half, conv_taps, out_grad, pw,
        far=(other, weight),
        sems=48,
        staged=True,
    )
    arrived = exchange(send, "seq")
    y, gp, sums = call(
        scan_kernel,
        7.0,
        None,
        [((SUB, 8, 128), F32)] * 2 + [((96, 8, 128), F32)],
        [((32, 8, 128), F32)] * 2,
        prod, gl, st, pw, res,
    )
    given = after(given, arrived, y)
    passed = lax.ppermute(given, ("seq", "chan"), joint_pairs("pass"))
    mixed_out, low = call(
        grads_kernel,
        8.0,
        at,
        [((128, ROWS), F32), ((ROWS + 32, 384), BF16)],
        [((SPAN, 128), F32), ((SPAN, 128), F32), ((EXT, 384), F32), ((EXT, 384), F32)]
        + [((EXT, 128), F32), ((EXT, 128), F32), ((48, 128), F32), ((EXT, 128), F32)]
        + [((32, 8, 128), F32)] * 4,
        arrived, pw, res, skip_gain[None, :], y, gp, sums, st, ext, conv_taps, out_grad,
        staged=True,
    )

    low_y = to_seq(low, 0, 1)
    low_core = to_chan(low, 0, 0, 1)
    terms = far_call(
        input_kernel,
        6.0,
        at,
        [((8, 256, ROWS), BF16)],
        [((2, ROWS, 384), BF16), ((768, ROWS), BF16), ((8, 2, 3, 256, 128), BF16), ((8, 256, ROWS), BF16)],
        26,
        low, low_core, weight, partner.reshape(weight.shape),
    )[0]
    pair_rows, half_rows = ((544, 384), BF16), ((HALF + 32, 384), BF16)
    one, one_back, four, four_back, near, middle, own_small = far_call(
        weight_kernel,
        40.0,
        at,
        [pair_rows] * 2 + [half_rows] * 2
        + [((2, 256, 384), F32), ((256, 384), F32), ((32, 384), BF16)],
        [((8, 2 * ROWS, 256), BF16), ((2, ROWS + 32, 384), BF16), ((2, 544, 384), BF16)]
        + [((2, HALF + 32, 384), BF16), ((3, 256, 384), F32)],
        28,
        mine, other, given, passed, low, low_y, terms,
    )
    terms = exchange(terms, "chan", CHIPS)
    four, four_back = to_seq(four, 2), to_seq(four_back, -2)
    one, one_back = to_seq(one, 1), to_seq(one_back, -1)
    back, ahead = call(
        relay_kernel,
        2.0,
        None,
        [((320, 384), BF16), ((288, 384), BF16)],
        [],
        near, one, four, one_back, four_back,
        staged=True,
    )
    back, ahead = to_seq(back, -2), to_seq(ahead, 2)
    input_grad = call(fold_input_kernel, 2.5, None, [((ROWS, 256), F32)], [], terms)[0]
    early = call(early_kernel, 2.0, None, [((256, 384), F32)], [], middle, one, one_back)[0]
    weight_grad, residue_grad, taps_grad, skip_grad = call(
        fold_kernel,
        2.5,
        at,
        [((3, 256, 128), F32), ((2, MODES, 128), F32), ((3, 3, 128), F32), ((1, 128), F32)],
        [((8, 16, 384), F32)],
        early, back, ahead, own_small, one, one_back, four, four_back,
        windows=((4, 512), (5, 512), (6, HALF), (7, HALF)),
        late=(input_grad,),
        staged=True,
    )
    return (mixed_out, input_grad, weight_grad, taps_grad, residue_grad, skip_grad.reshape(128))


def solution(mesh):
    in_specs = (
        P("seq", "chan"),
        P(None, None, "chan"),
        P(None, None, "chan"),
        P(None, "chan"),
        P(None, "chan"),
        P(None, None, "chan"),
        P("chan"),
        P("chan", "seq"),
    )
    out_specs = (
        P("chan", "seq"),
        P("seq", "chan"),
        P(None, "seq", "chan"),
        P(None, None, "chan"),
        P(None, None, "chan"),
        P("chan"),
    )
    return jax.shard_map(
        on_device, mesh=mesh, in_specs=in_specs, out_specs=out_specs, check_vma=False
    )
```

```python
import jax
import jax.numpy as jnp
from jax import lax
from jax.experimental import pallas as pl
from jax.experimental.pallas import tpu as pltpu
from jax.sharding import PartitionSpec as P

F32 = jnp.float32
BF16 = jnp.bfloat16
MODES = 16
SUB = 64
ROWS = 8 * SUB
EXT = ROWS + 8
SPAN = ROWS + SUB


def chan_pairs(dx, dy, dc):
    pairs = []
    for c in range(16):
        x, y, core = c // 4, c // 2 % 2, c % 2
        pairs.append((c, (x + dx) % 4 * 4 + (y + dy) % 2 * 2 + (core + dc) % 2))
    return pairs


def seq_pairs(dz, dy):
    return [(s, (s // 2 + dz) % 8 * 2 + (s % 2 + dy) % 2) for s in range(16)]


def to_chan(x, dx, dy, dc=0):
    return lax.ppermute(x, "chan", chan_pairs(dx, dy, dc))


def to_seq(x, dz, dy=0):
    return lax.ppermute(x, "seq", seq_pairs(dz, dy))


def pole_power(rate, angle, count):
    high = jnp.round(angle * 1024.0) * (1.0 / 1024.0)
    low = angle - high
    one, two = high * count, low * count
    mag = jnp.exp(-rate * count)
    cos1, sin1, cos2, sin2 = jnp.cos(one), jnp.sin(one), jnp.cos(two), jnp.sin(two)
    return mag * (cos1 * cos2 - sin1 * sin2), mag * (sin1 * cos2 + cos1 * sin2)


COUNTS = (1.0, -1.0, float(ROWS), float(ROWS - 1), float(ROWS - 2), float(SUB), float(2 * SUB), float(4 * SUB))


def halves(ref, row=None):
    if row is None:
        return ref[0:MODES, :], ref[MODES : 2 * MODES, :]
    return ref[row, 0:MODES, :], ref[row, MODES : 2 * MODES, :]


def fill(pw, rows, dst):
    for n in range(2 * MODES):
        line = rows[n : n + 1, :] if pw is None else pw[rows, n : n + 1, :]
        dst[n] = jnp.broadcast_to(line, (8, 128))


def sub_powers(pw, dst, back):
    place = lax.broadcasted_iota(jnp.int32, (8, 128), 0)
    place = 7 - place if back else place
    for n in range(MODES):
        re, im = jnp.ones((8, 128), F32), jnp.zeros((8, 128), F32)
        for level in range(3):
            here = (place >> level) & 1 == 1
            step = pw[5 + level, n : n + 1, :], pw[5 + level, MODES + n : MODES + n + 1, :]
            step = tuple(jnp.where(here, s, t) for s, t in zip(step, (1.0, 0.0)))
            re, im = times((re, im), step)
        dst[n] = re
        dst[MODES + n] = im


def times(a, b):
    return a[0] * b[0] - a[1] * b[1], a[0] * b[1] + a[1] * b[0]


def copy_all(pairs, sems):
    copies = [pltpu.make_async_copy(a, b, sems.at[i]) for i, (a, b) in enumerate(pairs)]
    for c in copies:
        c.start()
    return copies


def wait_all(copies, start=False):
    for c in copies:
        if start:
            c.start()
        c.wait()


def stream(sources, weight_far, par, held, weight, sems):
    copies = []
    for b in range(8):
        pairs = [(weight_far.at[:, b, par], weight.at[:, b])]
        pairs += [(src.at[b], dst.at[b]) for src, dst in zip(sources, held)]
        group = [pltpu.make_async_copy(f, t, sems.at[6 * b + i]) for i, (f, t) in enumerate(pairs)]
        for c in group:
            c.start()
        copies.append(group)
    return copies


def columns(weight, b):
    return jnp.concatenate([weight[k, b] for k in range(3)], axis=1)


def convolve(taps, ext, k):
    lanes = slice(128 * k, 128 * k + 128)
    total = taps[k, 0:1, :] * ext[8 : 8 + ROWS, lanes]
    total = total + taps[k, 1:2, :] * ext[7 : 7 + ROWS, lanes]
    return total + taps[k, 2:3, :] * ext[6 : 6 + ROWS, lanes]


def half_kernel(at, mine_far, weight_far, _, out, mine, weight, made, sems):
    copies = stream([mine_far], weight_far, at[0], [mine], weight, sems)
    for b in range(0, 8, 2):
        for i in range(b, b + 2):
            wait_all(copies[i])
        left = jnp.concatenate([mine[i] for i in range(b, b + 2)], axis=1)
        right = jnp.concatenate([columns(weight, i) for i in range(b, b + 2)], axis=0)
        total = jnp.dot(left, right, preferred_element_type=F32)
        made[...] = total if b == 0 else made[...] + total
    wait_all([pltpu.make_async_copy(made, out, sems.at[0])], start=True)


def states_kernel(
    at, other_far, weight_far, half, taps, og, pw,
    ext, prod, gl, st, send, other, weight, ends, lam, pwf, pwb, sems, io,
):
    seq = at[2]
    copies = stream([other_far], weight_far, 1 - at[0], [other], weight, sems)
    io.need(3)
    fill(pw, 0, lam)
    sub_powers(pw, pwf, True)
    sub_powers(pw, pwb, False)
    for b in range(0, 8, 2):
        for i in range(b, b + 2):
            wait_all(copies[i])
        left = jnp.concatenate([other[i] for i in range(b, b + 2)], axis=1)
        right = jnp.concatenate([columns(weight, i) for i in range(b, b + 2)], axis=0)
        total = jnp.dot(left, right, preferred_element_type=F32)
        if b == 0:
            io.need(0)
        ext[8:520, :] = (half[...] if b == 0 else ext[8:520, :]) + total
    ext[0:8, :] = jnp.zeros((8, 384), F32)
    ext[520:528, :] = jnp.zeros((8, 384), F32)
    io.done(0)
    io.need(1, 2)
    q, k, v = (convolve(taps, ext, i) for i in range(3))
    fresh = lax.broadcasted_iota(jnp.int32, (ROWS, 128), 0) >= 2
    prod[0:ROWS, :] = jnp.where(fresh, k * v, 0.0)
    cot = og[...].T
    gl[0:ROWS, :] = jnp.where(fresh, cot * q, 0.0)
    io.done(1, 2)
    edge = [k[0:2], v[0:2], q[0:2], cot[0:2]]
    edge += [ext[518:520, 128 * i : 128 * i + 128] for i in range(3)]
    edge = jnp.concatenate(edge + [jnp.zeros((2, 128), F32)], axis=0)
    half = MODES // 2
    for src, powers, back, base in ((prod, pwf, False, 0), (gl, pwb, True, 32)):
        for n0 in range(0, MODES, half):

            def body(step, carry, n0=n0, back=back, src=src):
                i = SUB - 1 - step if back else step
                v = src[pl.ds(i, 8, stride=SUB), :]
                out = []
                for k in range(half):
                    re, im = carry[2 * k], carry[2 * k + 1]
                    lr, li = lam[n0 + k], lam[MODES + n0 + k]
                    out += [re * lr - im * li + v, re * li + im * lr]
                return tuple(out)

            zero = tuple(jnp.zeros((8, 128), F32) for _ in range(2 * half))
            carry = lax.fori_loop(0, SUB, body, zero, unroll=4)
            for k in range(half):
                n = n0 + k
                re, im = carry[2 * k], carry[2 * k + 1]
                st[base + n] = re
                st[base + MODES + n] = im
                er, ei = times((re, im), (powers[n], powers[MODES + n]))
                ends[base + n : base + n + 1, :] = jnp.sum(er, axis=0, keepdims=True)
                ends[base + MODES + n : base + MODES + n + 1, :] = jnp.sum(ei, axis=0, keepdims=True)
    io.done(3)
    for j in range(16):
        send[j, 0:32, :] = jnp.where(j >= seq, ends[0:32, :], ends[32:64, :])
        send[j, 32:48, :] = edge


def scan_kernel(prod, gl, st, pw, res, y, gp, sums, lam, rho):
    fill(pw, 0, lam)
    fill(None, res, rho)
    half = MODES // 2
    place = lax.broadcasted_iota(jnp.int32, (8, 128), 0)
    for base, back in ((0, False), (32, True)):
        for n in range(MODES):

            def shift(v, by, back=back):
                moved = pltpu.roll(v, 8 - by if back else by, 0)
                return jnp.where(place < 8 - by if back else place >= by, moved, 0.0)

            re, im = shift(st[base + n], 1), shift(st[base + MODES + n], 1)
            for level, by in enumerate((1, 2, 4)):
                ar, ai = times(
                    (shift(re, by), shift(im, by)),
                    (pw[5 + level, n : n + 1, :], pw[5 + level, MODES + n : MODES + n + 1, :]),
                )
                re, im = re + ar, im + ai
            sums[32 + base + n] = re
            sums[32 + base + MODES + n] = im
    for n0 in range(0, MODES, half):

        def forward(step, carry, n0=n0):
            p = prod[pl.ds(step, 8, stride=SUB), :]
            g = gl[pl.ds(step, 8, stride=SUB), :]
            out = []
            total = None
            for k in range(half):
                re, im, sr, si = carry[4 * k : 4 * k + 4]
                lr, li = lam[n0 + k], lam[MODES + n0 + k]
                re, im = re * lr - im * li + p, re * li + im * lr
                term = re * rho[n0 + k] - im * rho[MODES + n0 + k]
                total = term if total is None else total + term
                out += [re, im, sr + g * re, si + g * im]
            y[step] = total if n0 == 0 else y[step] + total
            return tuple(out)

        zero = tuple(jnp.zeros((8, 128), F32) for _ in range(4 * half))
        carry = lax.fori_loop(0, SUB, forward, zero, unroll=4)
        for k in range(half):
            sums[n0 + k] = carry[4 * k + 2]
            sums[MODES + n0 + k] = carry[4 * k + 3]

        def backward(step, carry, n0=n0):
            i = SUB - 1 - step
            g = gl[pl.ds(i, 8, stride=SUB), :]
            out = []
            total = None
            for k in range(half):
                re, im = carry[2 * k : 2 * k + 2]
                lr, li = lam[n0 + k], lam[MODES + n0 + k]
                re, im = re * lr - im * li + g, re * li + im * lr
                term = re * rho[n0 + k] - im * rho[MODES + n0 + k]
                total = term if total is None else total + term
                out += [re, im]
            gp[i] = total if n0 == 0 else gp[i] + total
            return tuple(out)

        zero = tuple(jnp.zeros((8, 128), F32) for _ in range(2 * half))
        lax.fori_loop(0, SUB, backward, zero, unroll=4)


def grads_kernel(
    at, arrived, pw, res, skip, y, gp, sums, st, ext, taps, og_far,
    mixed, low, yt, gt, gb, br, prod, gl, small, og, lam, rho, pwf, pwb, io,
):
    seq = at[2]

    io.need(1, 2, 9)
    fill(pw, 0, lam)
    fill(None, res, rho)
    sub_powers(pw, pwf, True)
    sub_powers(pw, pwb, False)
    lam16, inv16, lam512, lam511, lam510 = (halves(pw, i) for i in range(5))
    rho16 = halves(res)
    io.need(0, 3)
    zero16 = jnp.zeros((MODES, 128), F32)
    s_in, u_in = (zero16, zero16), (zero16, zero16)
    zero2 = jnp.zeros((2, 128), F32)
    own = nxt = [zero2] * 6
    rim = [zero2] * 3
    first = lax.broadcasted_iota(jnp.int32, (2, 128), 0) == 0

    def choose(flag, new, old):
        return [jnp.where(flag, a, b) for a, b in zip(new, old)]

    before = [zero2] * 3
    for j in range(16):
        tilde = arrived[j, 32:40, :]
        kvq = []
        for k, rows in ((1, tilde[0:2]), (2, tilde[2:4]), (0, tilde[4:6])):
            t1, t2 = taps[k, 1:2, :], taps[k, 2:3, :]
            p2, p1 = before[k][0:1], before[k][1:2]
            kvq.append(rows + jnp.where(first, t1 * p1 + t2 * p2, t2 * p1))
        out_grad = tilde[6:8]
        product = kvq[0] * kvq[1]
        cotangent = out_grad * kvq[2]
        mine = kvq + [out_grad, product, cotangent]
        tail = arrived[j, 40:48, :]
        before = [tail[0:2], tail[2:4], tail[4:6]]
        own = choose(j == seq, mine, own)
        nxt = choose(j == seq + 1, mine, nxt)
        rim = choose(j == seq - 1, before, rim)
        got = halves(arrived, j)
        p0, p1 = product[0:1], product[1:2]
        g0, g1 = cotangent[0:1], cotangent[1:2]
        ahead = j < seq
        fixed = [
            got[i] + jnp.where(ahead, lam511[i] * p0 + lam510[i] * p1, lam16[i] * g1 + (g0 if i == 0 else 0.0))
            for i in range(2)
        ]
        re, im = times(fixed, halves(pw, 8 + j))
        behind = j > seq
        s_in = (s_in[0] + jnp.where(ahead, re, 0.0), s_in[1] + jnp.where(ahead, im, 0.0))
        u_in = (u_in[0] + jnp.where(behind, re, 0.0), u_in[1] + jnp.where(behind, im, 0.0))

    def read_out(state):
        return jnp.sum(rho16[0] * state[0] - rho16[1] * state[1], axis=0, keepdims=True)

    p0, p1, g0, g1 = own[4][0:1], own[4][1:2], own[5][0:1], own[5][1:2]
    x0 = times(lam16, s_in)
    x0 = (x0[0] + p0, x0[1])
    x1 = times(lam16, x0)
    x1 = (x1[0] + p1, x1[1])
    small[0:16, :] = g0 * x0[0] + g1 * x1[0]
    small[16:32, :] = -(g0 * x0[1] + g1 * x1[1])
    inv2 = times(inv16, inv16)
    s_in = tuple(s_in[i] + inv16[i] * p0 + inv2[i] * p1 for i in range(2))
    carried = times(lam512, s_in)
    last = halves(arrived, seq)
    last = (last[0] + carried[0], last[1] + carried[1])
    for extra in range(2):
        moved = times(lam16, last)
        last = (moved[0] + nxt[4][extra : extra + 1], moved[1])
        yt[ROWS + extra : ROWS + extra + 1, :] = read_out(last)
    gt[ROWS : ROWS + 1, :] = read_out(u_in)
    later = times(inv16, (u_in[0] - nxt[5][0:1], u_in[1]))
    gt[ROWS + 1 : ROWS + 2, :] = read_out(later)
    yt[ROWS + 2 : EXT, :] = jnp.zeros((EXT - ROWS - 2, 128), F32)
    gt[ROWS + 2 : EXT, :] = jnp.zeros((EXT - ROWS - 2, 128), F32)
    io.need(4, 5, 6, 7)

    half = MODES // 2
    for n0 in range(0, MODES, half):
        start_f, start_b = [], []
        for k in range(half):
            n = n0 + k
            l8 = (lam[n], lam[MODES + n])
            r8 = (rho[n], rho[MODES + n])

            def full(state, powers, base, n=n):
                wide = tuple(jnp.broadcast_to(s[n : n + 1, :], (8, 128)) for s in state)
                add = times(wide, (powers[n], powers[MODES + n]))
                return times((sums[base + n] + add[0], sums[base + MODES + n] + add[1]), l8)

            q = full(s_in, pwb, 32)
            rr, ri = times(q, (st[32 + n], st[48 + n]))
            small[n : n + 1, :] += jnp.sum(sums[n] + rr, axis=0, keepdims=True)
            small[MODES + n : MODES + n + 1, :] -= jnp.sum(sums[MODES + n] + ri, axis=0, keepdims=True)
            start_f += list(times(q, r8))
            start_b += list(times(full(u_in, pwf, 64), r8))

        def follow(src, dst, back, start, n0=n0):
            def body(step, carry):
                i = SUB - 1 - step if back else step
                at = pl.ds(i, 8, stride=SUB)
                total = src[i] if n0 == 0 else dst[at, :]
                out = []
                for k in range(half):
                    re, im = carry[2 * k], carry[2 * k + 1]
                    total = total + re
                    lr, li = lam[n0 + k], lam[MODES + n0 + k]
                    out += [re * lr - im * li, re * li + im * lr]
                dst[at, :] = total
                return tuple(out)

            lax.fori_loop(0, SUB, body, tuple(start), unroll=4)

        follow(y, yt, False, start_f)
        follow(gp, gt, True, start_b)

    none, one = (jnp.ones_like(zero16), zero16), lam16
    yt[0:1, :] -= read_out(inv16) * p1
    gt[0:1, :] += read_out(none) * g0 + read_out(one) * g1
    gt[1:2, :] += read_out(none) * g1

    io.need(8, 10)
    og[0:ROWS, :] = og_far[...].T
    og[ROWS + 2 : EXT, :] = jnp.zeros((EXT - ROWS - 2, 128), F32)
    for k in range(3):
        ext[6:8, 128 * k : 128 * k + 128] = rim[k]
    og[ROWS : ROWS + 2, :] = nxt[3]
    for k, at_k in ((0, 2), (1, 0), (2, 1)):
        lanes = slice(128 * k, 128 * k + 128)
        br[0:ROWS, lanes] = convolve(taps, ext, k)
        br[ROWS : ROWS + 2, lanes] = nxt[at_k]
    br[ROWS + 2 : EXT, :] = jnp.zeros((EXT - ROWS - 2, 384), F32)
    prod[...] = br[:, 128:256] * br[:, 256:384]
    gl[...] = og[...] * br[:, 0:128]
    gain = skip[...]
    long_out = yt[0:EXT, :] + gain * prod[...]
    gb[:, 0:128] = og[...] * long_out
    grad_prod = gt[0:EXT, :] + gain * gl[...]
    gb[:, 128:256] = grad_prod * br[:, 256:384]
    gb[:, 256:384] = grad_prod * br[:, 128:256]
    for k in range(3):
        lanes = slice(128 * k, 128 * k + 128)
        total = None
        for j in range(3):
            term = taps[k, j : j + 1, :] * gb[j : j + ROWS, lanes]
            total = term if total is None else total + term
            row = 32 + 3 * k + j
            small[row : row + 1, :] = jnp.sum(
                gb[0:ROWS, lanes] * ext[8 - j : 8 - j + ROWS, lanes], axis=0, keepdims=True
            )
        low[0:ROWS, lanes] = total.astype(BF16)
    small[41:42, :] = jnp.sum(gl[0:ROWS, :] * prod[0:ROWS, :], axis=0, keepdims=True)
    small[42:48, :] = jnp.zeros((6, 128), F32)
    wide = jnp.concatenate([small[16 * i : 16 * i + 16, :] for i in range(3)], axis=1)
    split_rows(wide, low, ROWS)
    io.done(1)
    mixed[...] = (br[0:ROWS, 0:128] * long_out[0:ROWS, :]).T


def split_rows(wide, dst, row):
    high = wide.astype(BF16)
    dst[row : row + 16, :] = high
    dst[row + 16 : row + 32, :] = (wide - high.astype(F32)).astype(BF16)


def join_rows(src, row):
    return src[row : row + 16, :].astype(F32) + src[row + 16 : row + 32, :].astype(F32)


def input_kernel(at, low, low_core, weight, partner, out, left, lturn, right, parts, sems):
    core = at[0]
    copies = copy_all([(low.at[0:ROWS], left.at[0]), (low_core.at[0:ROWS], left.at[1])], sems)
    far = []
    for n in range(8):
        for s, src in enumerate((weight, partner)):
            c = pltpu.make_async_copy(src.at[:, n, core], right.at[n, s], sems.at[2 + 2 * n + s])
            c.start()
            far.append(c)
    wait_all(copies)
    lturn[...] = jnp.concatenate([left[0].T, left[1].T], axis=0)
    sent = []
    for n in range(0, 8, 4):
        wait_all(far[2 * n : 2 * n + 8])
        cols = [
            jnp.concatenate([right[i, s, k] for s in range(2) for k in range(3)], axis=1)
            for i in range(n, n + 4)
        ]
        cols = jnp.concatenate(cols, axis=0)
        total = jnp.dot(cols, lturn[...], preferred_element_type=F32).astype(BF16)
        for i in range(4):
            parts[n + i] = total[256 * i : 256 * i + 256]
            c = pltpu.make_async_copy(parts.at[n + i], out.at[n + i], sems.at[18 + n + i])
            c.start()
            sent.append(c)
    wait_all(sent)


FAR_ORDER = (4, 3, -3, 1, -1, 2, -2, 0)
HALF = 128


def weight_kernel(at, mine, other, given, passed, low, low_y, _, *rest):
    outs, (held, cols, made, far_made, near_made, sems) = rest[:7], rest[7:]
    z = at[6]
    one, one_back, four, four_back, near, middle, own_small = outs
    far = []
    for n, d in enumerate(FAR_ORDER):
        p = lax.rem(z + (d + 8), 8)
        for s, pair in enumerate(((other, mine), (passed, given))):
            dst = held.at[n, ROWS * s : ROWS * s + ROWS]
            for flag, src in enumerate(pair):
                c = pltpu.make_async_copy(src.at[p], dst, sems.at[2 + 2 * n + s])

                @pl.when(at[3] == flag)
                def _(c=c):
                    c.start()

            far.append(c)
        if n == 0:
            copies = copy_all([(low, cols.at[0]), (low_y, cols.at[1])], sems)
    wait_all(copies)
    right = jnp.concatenate([cols[0, 0:ROWS, :], cols[1, 0:ROWS, :]], axis=0)
    wide = join_rows(cols.at[0], ROWS) + join_rows(cols.at[1], ROWS)
    for i in range(2):
        split_rows(wide, made.at[i], 512)
        split_rows(wide, far_made.at[i], HALF)
    sent = []

    def send(src, dst):
        c = pltpu.make_async_copy(src, dst, sems.at[18 + len(sent)])
        c.start()
        sent.append(c)

    send(made.at[0, 512:544], own_small)
    for n, d in enumerate(FAR_ORDER):
        if n % 2 == 0:
            wait_all(far[2 * n : 2 * n + 4])
            both = jnp.concatenate([held[n], held[n + 1]], axis=1)
            both = lax.dot_general(both, right, (((0,), (0,)), ((), ())), preferred_element_type=F32)
        total = both[256 * (n % 2) : 256 * (n % 2) + 256]
        if n == 0:
            total = total.astype(BF16)
            far_made[0, 0:HALF, :] = total[HALF:]
            far_made[1, 0:HALF, :] = total[0:HALF]
            send(far_made.at[0], four)
            send(far_made.at[1], four_back)
        elif n < 5:
            row = 0 if n < 3 else 256
            made[(n - 1) % 2, row : row + 256, :] = total.astype(BF16)
            if n >= 3:
                send(made.at[n - 3], (one, one_back)[n - 3])
        else:
            near_made[n - 5] = total
            send(near_made.at[n - 5], middle if n == 7 else near.at[n - 5])
    wait_all(sent)


def relay_kernel(near, one, four, one_back, four_back, back, ahead, io):
    io.need(0, 3, 4)
    total = near[1] + one_back[0:256, :].astype(F32)
    back[0:HALF, :] = (total[0:HALF] + four_back[0:HALF, :].astype(F32)).astype(BF16)
    back[HALF:256, :] = total[HALF:].astype(BF16)
    back[256:288, :] = one_back[512:544, :]
    back[288:320, :] = four_back[HALF : HALF + 32, :]
    io.done(0)
    io.need(1, 2)
    total = near[0] + one[0:256, :].astype(F32)
    ahead[0:HALF, :] = total[0:HALF].astype(BF16)
    ahead[HALF:256, :] = (total[HALF:] + four[0:HALF, :].astype(F32)).astype(BF16)
    ahead[256:288, :] = one[512:544, :]


def fold_input_kernel(parts, out):
    total = parts[0].astype(F32)
    for j in range(1, 8):
        total = total + parts[j].astype(F32)
    out[...] = total.T


def early_kernel(middle, one, one_back, out):
    out[...] = middle[...] + one[256:512, :].astype(F32) + one_back[256:512, :].astype(F32)


def fold_kernel(
    at, early, back, ahead, own_small, one, one_back, four, four_back, out, res, taps, skip, table, io
):
    z = at[6]
    io.need(0, 1, 2)
    total = early[...] + back[0:256, :].astype(F32) + ahead[0:256, :].astype(F32)
    for k in range(3):
        out[k] = total[:, 128 * k : 128 * k + 128]
    io.done(0)
    io.need(3, 4, 5, 6, 7)
    came = ((own_small, 0, 0), (one, 0, -1), (four, 0, -2), (ahead, 256, -3))
    came += ((one_back, 0, 1), (four_back, 0, 2), (back, 256, 3), (back, 288, 4))
    for src, row, d in came:
        table[lax.rem(z + (d + 8), 8)] = join_rows(src, row)
    wide = table[0]
    for j in range(1, 8):
        wide = wide + table[j]
    res[0] = wide[:, 0:128]
    res[1] = wide[:, 128:256]
    for k in range(3):
        taps[k] = wide[3 * k : 3 * k + 3, 256:384]
    skip[...] = wide[9:10, 256:384]


VMEM_BYTES = 64 * 1024 * 1024 - 128 * 1024
FAR = pl.BlockSpec(memory_space=pltpu.HBM)
SCALARS = pl.BlockSpec(memory_space=pltpu.SMEM)


def raw_call(kernel, us, outs, scratch, sems, args, in_specs, out_specs):
    return pl.pallas_call(
        kernel,
        in_specs=in_specs,
        out_specs=out_specs,
        out_shape=[jax.ShapeDtypeStruct(s, t) for s, t in outs],
        scratch_shapes=[pltpu.VMEM(s, t) for s, t in scratch] + [pltpu.SemaphoreType.DMA((sems,))],
        compiler_params=pltpu.CompilerParams(vmem_limit_bytes=VMEM_BYTES),
        cost_estimate=pl.CostEstimate(flops=int(us * 1.1e9), bytes_accessed=0, transcendentals=0),
    )(*args)


def far_call(kernel, us, at, outs, scratch, sems, *args):
    scalars = () if at is None else (at,)
    specs = [SCALARS] * len(scalars) + [FAR] * len(args)
    return raw_call(kernel, us, outs, scratch, sems, scalars + args, specs, [FAR] * len(outs))


class Staged:
    def __init__(self, ins, outs):
        self.ins, self.outs, self.here, self.gone = ins, outs, set(), set()

    def need(self, *which):
        for i in which:
            if i not in self.here:
                self.here.add(i)
                self.ins[i].wait()

    def done(self, *which):
        for i in which:
            if i not in self.gone:
                self.gone.add(i)
                self.outs[i].start()


def call(kernel, us, at, outs, scratch, *args, far=(), sems=0, late=(), staged=False, windows=()):
    scalars = () if at is None else (at,)
    n_s, n_f, n_i, n_l, n_o = len(scalars), len(far), len(args), len(late), len(outs)

    def body(*refs):
        refs = list(refs)

        def take(count):
            head = refs[:count]
            del refs[:count]
            return head

        top, far_refs, ins, _, results = take(n_s), take(n_f), take(n_i), take(n_l), take(n_o)
        held, made, own, sem = take(n_i), take(n_o), refs[:-1], refs[-1]

        def copies(pairs, base):
            return [pltpu.make_async_copy(a, b, sem.at[base + i]) for i, (a, b) in enumerate(pairs)]

        for i, row in windows:
            ins[i] = ins[i].at[row : row + 32]
        coming = copies(zip(ins, held), sems)
        for c in coming:
            c.start()
        io = Staged(coming, copies(zip(made, results), sems + n_i))
        if not staged:
            io.need(*range(n_i))
        extra = ((sem,) if far else ()) + ((io,) if staged else ())
        kernel(*top, *far_refs, *held, *made, *own, *extra)
        io.need(*range(n_i))
        io.done(*range(n_o))
        wait_all(io.outs)

    shapes = [(a.shape, a.dtype) for a in args]
    for i, _ in windows:
        shapes[i] = ((32, args[i].shape[1]), args[i].dtype)
    buffers = shapes + list(outs) + list(scratch)
    specs = [SCALARS] * n_s + [FAR] * (n_f + n_i + n_l)
    total = sems + n_i + n_o
    return raw_call(
        body, us, outs, buffers, total, scalars + tuple(far) + args + tuple(late), specs, [FAR] * n_o
    )


def after(x, *deps):
    return pl.pallas_call(
        lambda *_: None,
        in_specs=[pl.BlockSpec(memory_space=pl.ANY)] * (1 + len(deps)),
        out_specs=pl.BlockSpec(memory_space=pl.ANY),
        out_shape=jax.ShapeDtypeStruct(x.shape, x.dtype),
        input_output_aliases={0: 0},
    )(x, *deps)


CHIPS = [[x * 4 + y * 2 + c for x in range(4) for y in range(2)] for c in range(2)]
COLUMNS = [[z * 2 + y for z in range(8)] for y in range(2)]


def exchange(x, axis, groups=None):
    return lax.all_to_all(
        x, axis, split_axis=0, concat_axis=0, tiled=True, axis_index_groups=groups
    )


def joint_pairs(kind):
    pairs = []
    for s in range(16):
        for c in range(16):
            wanted = s % 2 == c % 2
            if kind == "give" and not wanted:
                pairs.append((s * 16 + c, (s ^ 1) * 16 + c))
            if kind == "pass" and wanted:
                pairs.append((s * 16 + c, s * 16 + (c ^ 1)))
    return pairs


def on_device(
    hidden_in, in_weight, conv_taps, decay_rate, mode_angle, residue, skip_gain, out_grad
):
    chan, seq = lax.axis_index("chan"), lax.axis_index("seq")
    core, yl = chan % 2, seq % 2
    same = (yl == core).astype(jnp.int32)
    at = jnp.stack([core, chan, seq, same, chan // 4, chan // 2 % 2, seq // 2]).astype(jnp.int32)

    mine = exchange(jnp.broadcast_to(hidden_in[None], (8, ROWS, 256)), "chan", CHIPS)
    partner = to_chan(in_weight, 0, 0, 1)

    away = jnp.abs(jnp.arange(16, dtype=jnp.int32) - seq).astype(F32) - 1.0
    counts = jnp.concatenate([jnp.array(COUNTS, F32), jnp.maximum(away, 0.0) * float(ROWS)])
    pw = pole_power(decay_rate[None], mode_angle[None], counts[:, None, None])
    pw = jnp.concatenate(pw, axis=1)
    res = residue.reshape(2 * MODES, 128)

    other = to_chan(mine, 0, 0, 1)
    weight = in_weight.reshape(3, 8, 2, 256, 128)
    block, wblock = ((8, ROWS, 256), BF16), ((3, 8, 256, 128), BF16)
    half = far_call(
        half_kernel, 4.0, at, [((ROWS, 384), F32)], [block, wblock, ((ROWS, 384), F32)], 48, mine, weight, pw
    )[0]
    given = lax.ppermute(mine, ("seq", "chan"), joint_pairs("give"))
    ext, prod, gl, st, send = call(
        states_kernel,
        8.0,
        at,
        [((528, 384), F32), ((SPAN, 128), F32), ((SPAN, 128), F32), ((64, 8, 128), F32), ((16, 48, 128), F32)],
        [block, wblock, ((64, 128), F32)] + [((32, 8, 128), F32)] * 3,
        half, conv_taps, out_grad, pw,
        far=(other, weight),
        sems=48,
        staged=True,
    )
    arrived = exchange(send, "seq")
    y, gp, sums = call(
        scan_kernel,
        7.0,
        None,
        [((SUB, 8, 128), F32)] * 2 + [((96, 8, 128), F32)],
        [((32, 8, 128), F32)] * 2,
        prod, gl, st, pw, res,
    )
    given = after(given, arrived, y)
    passed = lax.ppermute(given, ("seq", "chan"), joint_pairs("pass"))
    mixed_out, low = call(
        grads_kernel,
        8.0,
        at,
        [((128, ROWS), F32), ((ROWS + 32, 384), BF16)],
        [((SPAN, 128), F32), ((SPAN, 128), F32), ((EXT, 384), F32), ((EXT, 384), F32)]
        + [((EXT, 128), F32), ((EXT, 128), F32), ((48, 128), F32), ((EXT, 128), F32)]
        + [((32, 8, 128), F32)] * 4,
        arrived, pw, res, skip_gain[None, :], y, gp, sums, st, ext, conv_taps, out_grad,
        staged=True,
    )

    low_y = to_seq(low, 0, 1)
    low_core = to_chan(low, 0, 0, 1)
    terms = far_call(
        input_kernel,
        6.0,
        at,
        [((8, 256, ROWS), BF16)],
        [((2, ROWS, 384), BF16), ((768, ROWS), BF16), ((8, 2, 3, 256, 128), BF16), ((8, 256, ROWS), BF16)],
        26,
        low, low_core, weight, partner.reshape(weight.shape),
    )[0]
    pair_rows, half_rows = ((544, 384), BF16), ((HALF + 32, 384), BF16)
    one, one_back, four, four_back, near, middle, own_small = far_call(
        weight_kernel,
        40.0,
        at,
        [pair_rows] * 2 + [half_rows] * 2
        + [((2, 256, 384), F32), ((256, 384), F32), ((32, 384), BF16)],
        [((8, 2 * ROWS, 256), BF16), ((2, ROWS + 32, 384), BF16), ((2, 544, 384), BF16)]
        + [((2, HALF + 32, 384), BF16), ((3, 256, 384), F32)],
        28,
        mine, other, given, passed, low, low_y, terms,
    )
    terms = exchange(terms, "chan", CHIPS)
    four, four_back = to_seq(four, 2), to_seq(four_back, -2)
    one, one_back = to_seq(one, 1), to_seq(one_back, -1)
    back, ahead = call(
        relay_kernel,
        2.0,
        None,
        [((320, 384), BF16), ((288, 384), BF16)],
        [],
        near, one, four, one_back, four_back,
        staged=True,
    )
    back, ahead = to_seq(back, -2), to_seq(ahead, 2)
    input_grad = call(fold_input_kernel, 2.5, None, [((ROWS, 256), F32)], [], terms)[0]
    early = call(early_kernel, 2.0, None, [((256, 384), F32)], [], middle, one, one_back)[0]
    weight_grad, residue_grad, taps_grad, skip_grad = call(
        fold_kernel,
        2.5,
        at,
        [((3, 256, 128), F32), ((2, MODES, 128), F32), ((3, 3, 128), F32), ((1, 128), F32)],
        [((8, 16, 384), F32)],
        early, back, ahead, own_small, one, one_back, four, four_back,
        windows=((4, 512), (5, 512), (6, HALF), (7, HALF)),
        late=(input_grad,),
        staged=True,
    )
    return (mixed_out, input_grad, weight_grad, taps_grad, residue_grad, skip_grad.reshape(128))


def solution(mesh):
    in_specs = (
        P("seq", "chan"),
        P(None, None, "chan"),
        P(None, None, "chan"),
        P(None, "chan"),
        P(None, "chan"),
        P(None, None, "chan"),
        P("chan"),
        P("chan", "seq"),
    )
    out_specs = (
        P("chan", "seq"),
        P("seq", "chan"),
        P(None, "seq", "chan"),
        P(None, None, "chan"),
        P(None, None, "chan"),
        P("chan"),
    )
    return jax.shard_map(
        on_device, mesh=mesh, in_specs=in_specs, out_specs=out_specs, check_vma=False
    )
```
